32 devices in a mesh: tile: 16 (over z, y, x), mem: 2 (over core).
Axes of the slice: x: 2, y: 2, z: 4, core: 2. Of those that a mesh axis runs over, the one named last changes fastest.
Arguments:
- inc_fine: bfloat16 [6, 196608], P(None, 'tile'), may hold values from -8 to 11
- pair_owner: int32 [384, 4], P('tile'), may hold values from 0 to 15, all different within a row; in each aligned block of 24 rows (0 to 23, 24 to 47, ...) at most 12 rows name the same one
- pair_block: int32 [384, 4], P('tile'), may hold values from 0 to 95
- pair_count: int32 [384, 4], P('tile'), may hold values from 1 to 128
- pair_weight: bfloat16 [384, 4, 128, 128], P('tile'), may hold values from 0.049804688 to 1
- cell_area: float32 [49152], P('tile'), may hold values from 0.07 to 5.6
- prior: bfloat16 [6, 80, 49152], P(None, 'mem', 'tile'), may hold values from -6 to 6
- posterior: bfloat16 [6, 80, 49152], P(None, 'mem', 'tile'), may hold values from -4 to 4
Outputs:
- analysis: bfloat16 [6, 80, 49152], P(None, 'mem', 'tile')
The draws below stay inside these ranges and needn't reach their ends.
Inputs may be any that keep to these rules, and one draw needn't show every extreme that they name: `pair_owner`: among the 24 rows of one device (aligned blocks) no owner is named more than 12 times, a bound that some block reaches; the 4 owners of a row differ.
All inputs are finite; a program needn't handle non-finite values.
Results may differ from the reference program's by a relative error of at most 0.0006.
Values may be sent and summed in bfloat16 or wider, within the bound.
A program may use at most 64 MiB of HBM per device.

```python
import math
import jax
import jax.numpy as jnp
import numpy as np
from jax import lax

CHANNELS = 6
MEMBERS = 80
BLOCK = 128
PAIRS = 4
CBLOCKS = 24
FBLOCKS = 96
SLOTS = 12
COARSE = 49152
FINE = 196608
ALL_BLOCKS = 384
N_TILE = 16


def draw_inc_fine(key, part):
    key = jax.random.fold_in(key, 11)
    key_rough, key_level = jax.random.split(key, 2)
    position = jnp.arange(FINE, dtype=jnp.float32) / FINE
    rough = 2.0 * jax.random.truncated_normal(key_rough, -4.0, 4.0, (CHANNELS, FINE), jnp.float32)
    level = jax.random.uniform(key_level, (CHANNELS, 1), jnp.float32, 0.5, 1.0)
    return (level * (1.0 + 2.0 * position)[None, :] + rough).astype(jnp.bfloat16)


def draw_cell_area(key, part):
    key = jax.random.fold_in(key, 23)
    key_trend, key_spread = jax.random.split(key, 2)
    position = jnp.arange(COARSE, dtype=jnp.float32) / COARSE
    slope = jax.random.uniform(key_trend, (), jnp.float32, -2.3, 2.3)
    trend = jnp.exp(slope * (position - 0.5))
    spread = jax.random.uniform(key_spread, (COARSE,), jnp.float32, 0.5, 1.5)
    return trend * spread


def touch_ends(entries, own_key, low, top_value):
    longest = entries.shape.index(max(entries.shape))
    spots = []
    for shift in (0, 1):
        where = [jax.random.randint(jax.random.fold_in(own_key, axis), (), 0, length) for axis, length in enumerate(entries.shape)]
        where[longest] = (where[longest] + shift) % entries.shape[longest]
        spots.append(tuple(where))
    return entries.at[spots[0]].set(low).at[spots[1]].set(top_value)


def block_scale(key, extent, pieces, least, high):
    factor_of, own = 1.0, jax.random.fold_in(key, 6)
    for axis_at, parts in pieces:
        draws = jnp.exp(jax.random.uniform(jax.random.fold_in(own, axis_at), (parts,), jnp.float32, least / len(pieces), high / len(pieces)))
        factor_of = factor_of * jnp.repeat(draws, extent[axis_at] // parts).reshape([-1 if axis == axis_at else 1 for axis in range(len(extent))])
    return factor_of


def routed_block(own_key, own, number, rows, number_of, top, reach, skew):
    sequence = jax.random.permutation(own_key, number_of)
    crowded, usual = portions_of(number_of, rows * top, reach, skew, True), portions_of(number_of, rows * top, reach, skew, False)
    places = jnp.arange(number_of)

    def named(sizes, rotation):
        used = int((sizes > 0).sum())
        fixed = max(1, used // 4)
        shifted = fixed + (places - fixed + rotation * (used - fixed)) % max(1, number_of - fixed)
        return jnp.zeros((number_of,), jnp.int32).at[sequence[jnp.where(places < fixed, places, shifted)]].set(jnp.asarray(sizes, jnp.int32))

    sizes = jnp.where(number % 4 == 0, named(crowded, number // 4), named(usual, number - number // 4 - 1))
    mixed = jax.random.permutation(jax.random.fold_in(own, 3), number_of)
    source_of, sink = mixed[0:number_of // 2 * 2:2], mixed[1:number_of // 2 * 2:2]
    margin = jnp.minimum(sizes[source_of] - 1, reach - sizes[sink]) // 2
    margin = jnp.where((source_of == sequence[0]) | (sink == sequence[0]) | (sizes[sink] == 0), 0, jnp.maximum(margin, 0))
    shifted = jax.random.randint(jax.random.fold_in(own, 4), (number_of // 2,), 0, 1 << 20) % (margin + 1)
    sizes = sizes.at[source_of].add(-shifted).at[sink].add(shifted)
    members = jnp.searchsorted(jnp.cumsum(sizes), jnp.arange(rows * top), side="right").astype(jnp.int32)
    listing = members.reshape(top, rows).T
    listing = listing[jax.random.permutation(jax.random.fold_in(own, 1), rows)]
    rotation = jax.random.randint(jax.random.fold_in(own, 2), (rows, 1), 0, top)
    return jnp.take_along_axis(listing, (jnp.arange(top)[None, :] + rotation) % top, axis=1)


def portions_of(amount, total, limit, skew, full):
    weights = [(1 << 20) // math.isqrt(rank ** skew) + 1 for rank in range(1, amount + 1)]
    largest = limit if full else min(limit, max(-(-total // amount), total * weights[0] // sum(weights)))
    least = 1 if total - largest >= amount - 1 else 0
    given, surplus = [largest] + [least] * (amount - 1), total - largest - least * (amount - 1)
    while surplus > 0:
        candidates = [i for i in range(1, amount) if given[i] < largest] or [i for i in range(1, amount) if given[i] < limit]
        mass, budget = sum([weights[i] for i in candidates]), surplus
        for i in candidates:
            more = min(limit - given[i], max(1, budget * weights[i] // mass), surplus)
            given[i] = given[i] + more
            surplus = surplus - more
    return np.array(given)


def noise(own_key, dims, width, limit, pieces=(), kind=jnp.bfloat16):
    gain = block_scale(own_key, dims, pieces, -0.22, 0.18) if pieces else 1.0
    entries = jax.random.normal(own_key, dims, jnp.float32) * width * gain
    return jnp.minimum(jnp.maximum(entries, -limit), limit).astype(kind)


def setup_inputs(seed: int = 0) -> dict:
    key_list = jax.random.split(jax.random.key(seed), 9)
    inc_fine = draw_inc_fine(jax.random.fold_in(key_list[8], 71), 0)
    pair_owner_keys = jax.random.split(jax.random.fold_in(key_list[1], 1), ALL_BLOCKS // CBLOCKS)
    pair_owner_turns = jax.random.permutation(jax.random.fold_in(key_list[1], 3), ALL_BLOCKS // CBLOCKS)
    pair_owner = jax.vmap(lambda own, number: routed_block(jax.random.fold_in(key_list[1], 2), own, number, CBLOCKS, N_TILE, PAIRS, SLOTS, 2))(pair_owner_keys, pair_owner_turns).reshape((ALL_BLOCKS, PAIRS))
    pair_block = touch_ends(jax.random.randint(key_list[2], (ALL_BLOCKS, PAIRS), 0, FBLOCKS), jax.random.fold_in(key_list[2], 1), 0, FBLOCKS - 1).astype(jnp.int32)
    pair_count = touch_ends(jax.random.randint(key_list[3], (ALL_BLOCKS, PAIRS), 1, BLOCK + 1), jax.random.fold_in(key_list[3], 1), 1, BLOCK).astype(jnp.int32)
    pair_weight = jnp.clip(0.049804688 + 0.9501953 * jax.random.uniform(key_list[4], (ALL_BLOCKS, PAIRS, BLOCK, BLOCK), jnp.float32) ** block_scale(key_list[4], (ALL_BLOCKS, PAIRS, BLOCK, BLOCK), ((0, 16),), -0.2, 0.2), 0.049804688, 1.0).astype(jnp.bfloat16)
    cell_area = draw_cell_area(jax.random.fold_in(key_list[8], 71), 0)
    prior = noise(key_list[6], (CHANNELS, MEMBERS, COARSE), 1.0, 6.0, ((1, 2), (2, 16)))
    posterior = noise(key_list[7], (CHANNELS, MEMBERS, COARSE), 0.6, 4.0, ((1, 2), (2, 16)))
    return dict(inc_fine=inc_fine, pair_owner=pair_owner, pair_block=pair_block, pair_count=pair_count, pair_weight=pair_weight, cell_area=cell_area, prior=prior, posterior=posterior)


relax_weight = 0.85
variance_eps = 1e-06

def reference(inc_fine, pair_owner, pair_block, pair_count, pair_weight, cell_area, prior, posterior):
    channels = inc_fine.shape[0]
    fine_rows = inc_fine.reshape(channels, -1, BLOCK)
    source = (pair_owner * FBLOCKS + pair_block).reshape(-1).astype(jnp.int32)
    picked = jnp.take(fine_rows, source, axis=1).reshape(channels, ALL_BLOCKS, PAIRS, BLOCK)
    live = jnp.arange(BLOCK, dtype=jnp.int32)[None, None, :] < pair_count[:, :, None]
    masked = jnp.where(live[:, :, None, :], pair_weight, jnp.zeros((), pair_weight.dtype))
    weight_total = lax.optimization_barrier(jnp.sum(masked.astype(jnp.float32), axis=(1, 3)))
    weighted = jnp.einsum('rpij,krpj->kri', masked.astype(jnp.float32), picked.astype(jnp.float32), precision=lax.Precision.HIGHEST)
    coarse = (weighted / weight_total[None]).reshape(channels, COARSE)
    level_mean = lax.optimization_barrier(jnp.sum(coarse * cell_area[None, :], axis=1)) / jnp.sum(cell_area)
    increment = coarse - level_mean[:, None]
    prior_wide = prior.astype(jnp.float32)
    post_wide = posterior.astype(jnp.float32)
    prior_mean = lax.optimization_barrier(jnp.sum(prior_wide, axis=1)) / MEMBERS
    post_mean = lax.optimization_barrier(jnp.sum(post_wide, axis=1)) / MEMBERS
    prior_dev = prior_wide - prior_mean[:, None, :]
    post_dev = post_wide - post_mean[:, None, :]
    prior_spread = jnp.sqrt(lax.optimization_barrier(jnp.sum(prior_dev * prior_dev, axis=1)) / (MEMBERS - 1) + variance_eps)
    post_spread = jnp.sqrt(lax.optimization_barrier(jnp.sum(post_dev * post_dev, axis=1)) / (MEMBERS - 1) + variance_eps)
    factor = 1.0 + relax_weight * (prior_spread - post_spread) / post_spread
    center = prior_mean + increment
    return (center[:, None, :] + factor[:, None, :] * post_dev).astype(jnp.bfloat16)
```

```python
import functools

import jax
import jax.numpy as jnp
from jax import lax
from jax.experimental import pallas as pl
from jax.experimental.pallas import tpu as pltpu
from jax.sharding import PartitionSpec as P

relax_weight = 0.85
variance_eps = 1e-06
f32 = jnp.float32
bf16 = jnp.bfloat16
MESH = pl.DeviceIdType.MESH
LANES = 128
SUB = 8
ONES = 7


def round_up(n, k):
    return -(-n // k) * k


def kernel(
    tiles,
    mems,
    cap,
    inc_ref,
    owner_ref,
    block_ref,
    count_ref,
    area_ref,
    weight_hbm,
    prior_hbm,
    post_hbm,
    out_ref,
    weight,
    prior,
    post,
    tall,
    fine,
    before,
    square,
    hits,
    ask,
    asked,
    pick,
    served,
    got,
    spread,
    stats,
    coarse,
    level,
    local_sem,
    ask_send,
    ask_recv,
    data_send,
    data_recv,
    stat_send,
    stat_recv,
    coarse_send,
    coarse_recv,
    level_send,
    level_recv,
):
    channels = inc_ref.shape[0]
    rows, pairs = owner_ref.shape
    fblocks = inc_ref.shape[1] // LANES
    fine_pad = fine.shape[0]
    part = got.shape[1] // LANES
    slots = got.shape[0] // tiles
    row_pad = pick.shape[0] // pairs
    members, cells = prior.shape[1], prior.shape[2]
    devices = tiles * mems
    me = lax.axis_index("tile")
    core = lax.axis_index("mem")
    flat = me * mems + core
    first = jnp.minimum(core * part, channels - part)

    barrier = pltpu.get_barrier_semaphore()

    def greet(k, carry):
        other = lax.rem(flat + k, devices)
        pl.semaphore_signal(
            barrier, inc=1, device_id=(other // mems, lax.rem(other, mems)), device_id_type=MESH
        )
        return carry

    lax.fori_loop(1, devices, greet, 0)
    load_prior = pltpu.make_async_copy(prior_hbm, prior, local_sem.at[0])
    load_post = pltpu.make_async_copy(post_hbm, post, local_sem.at[1])
    load_weight = pltpu.make_async_copy(weight_hbm, weight, local_sem.at[2])
    load_prior.start()
    load_post.start()
    load_weight.start()

    lane = lax.broadcasted_iota(jnp.int32, (rows, LANES), 1)
    owner = owner_ref[...]
    block = block_ref[...]
    named = [owner[:, p : p + 1] == lane for p in range(pairs)]
    any_named = jnp.zeros((rows, LANES), f32)
    wanted = jnp.zeros((rows, LANES), f32)
    for p in range(pairs):
        any_named = any_named + jnp.where(named[p], 1.0, 0.0)
        wanted = wanted + jnp.where(named[p], (block[:, p : p + 1] + 1).astype(f32), 0.0)
    run = jnp.zeros((1, LANES), f32)
    for r in range(rows):
        before[r : r + 1, :] = run
        run = run + any_named[r : r + 1, :]
    earlier = before[...]
    square[...] = jnp.zeros_like(square)
    for s in range(cap):
        chosen = jnp.where((earlier == float(s)) & (any_named > 0.0), wanted, 0.0)
        square[s : s + 1, :] = jnp.sum(chosen, axis=0, keepdims=True)
    turned = jnp.transpose(square[...]) - 1.0
    for t in range(tiles):
        ask[t] = turned[t : t + 1, :]

    pl.semaphore_wait(barrier, devices - 1)

    def ask_copy(k, here):
        other = lax.rem(me + k, tiles)
        return pltpu.make_async_remote_copy(
            src_ref=ask.at[other],
            dst_ref=asked.at[here if here is not None else other],
            send_sem=ask_send.at[other],
            recv_sem=ask_recv.at[here if here is not None else other],
            device_id=(other, core),
            device_id_type=MESH,
        )

    def start_ask(k, carry):
        ask_copy(k, me).start()
        return carry

    lax.fori_loop(1, tiles, start_ask, 0)
    asked[pl.ds(me, 1)] = ask[pl.ds(me, 1)]

    for b in range(fblocks):
        tall[b * SUB : b * SUB + channels, :] = inc_ref[:, b * LANES : (b + 1) * LANES].astype(f32)
    fine[...] = jnp.zeros_like(fine)
    planes = [tall[pl.ds(c, fblocks, stride=SUB), :] for c in range(channels)]
    for k in range(part):
        value = planes[k]
        for c in range(1, channels):
            value = jnp.where(first + k == c, planes[c], value)
        fine[:fblocks, k * LANES : (k + 1) * LANES] = value.astype(bf16)

    wide = lax.broadcasted_iota(jnp.int32, (rows, tiles * slots), 1).astype(f32)
    pick[...] = jnp.zeros_like(pick)
    for p in range(pairs):
        slot = jnp.sum(jnp.where(named[p], earlier, 0.0), axis=1, keepdims=True)
        place = owner[:, p : p + 1].astype(f32) * float(slots) + slot
        pick[p * row_pad : p * row_pad + rows, :] = jnp.where(wide == place, 1.0, 0.0).astype(bf16)

    chunk = next(n for n in (512, 384, 256, 128) if cells % n == 0)
    sub = lax.broadcasted_iota(jnp.int32, (SUB, chunk), 0)

    def member_stats(ref, base):
        def body(j, carry):
            at = pl.ds(pl.multiple_of(j * chunk, chunk), chunk)
            sums = jnp.zeros((SUB, chunk), f32)
            squares = jnp.zeros((SUB, chunk), f32)
            for c in range(channels):
                values = ref[c, :, at].astype(f32)
                total = jnp.sum(values, axis=0, keepdims=True)
                dev = values - total * (1.0 / members)
                sq = jnp.sum(dev * dev, axis=0, keepdims=True)
                sums = jnp.where(sub == c, total, sums)
                squares = jnp.where(sub == c, sq, squares)
            stats[core, base : base + SUB, at] = sums
            stats[core, base + SUB : base + 2 * SUB, at] = squares
            return carry

        lax.fori_loop(0, cells // chunk, body, 0)

    load_prior.wait()
    member_stats(prior, 0)

    def wait_ask(k, carry):
        ask_copy(k, None).wait()
        return carry

    lax.fori_loop(1, tiles, wait_ask, 0)
    square[...] = jnp.zeros_like(square)
    for t in range(tiles):
        square[t : t + 1, :] = asked[t]
    turned = jnp.transpose(square[...])
    fine_lane = lax.broadcasted_iota(jnp.int32, (slots, fine_pad), 1).astype(f32)
    for t in range(tiles):
        hits[t * slots : (t + 1) * slots, :] = jnp.where(
            turned[:slots, t : t + 1] == fine_lane, 1.0, 0.0
        ).astype(bf16)
    served[...] = jnp.dot(hits[...], fine[...], preferred_element_type=f32).astype(bf16)

    def rows_of(t):
        return pl.ds(pl.multiple_of(t * slots, slots), slots)

    def data_copy(k, here):
        other = lax.rem(me + k, tiles)
        source = here if here is not None else other
        return pltpu.make_async_remote_copy(
            src_ref=served.at[rows_of(other)],
            dst_ref=got.at[rows_of(source)],
            send_sem=data_send.at[other],
            recv_sem=data_recv.at[source],
            device_id=(other, core),
            device_id_type=MESH,
        )

    def start_data(k, carry):
        data_copy(k, me).start()
        return carry

    lax.fori_loop(1, tiles, start_data, 0)
    got[rows_of(me), :] = served[rows_of(me), :]

    load_post.wait()
    member_stats(post, 2 * SUB)

    def core_copy(buffer, send, recv, k, here):
        other = lax.rem(core + k, mems)
        source = here if here is not None else other
        return pltpu.make_async_remote_copy(
            src_ref=buffer.at[core],
            dst_ref=buffer.at[source],
            send_sem=send.at[other],
            recv_sem=recv.at[source],
            device_id=(me, other),
            device_id_type=MESH,
        )

    for k in range(1, mems):
        core_copy(stats, stat_send, stat_recv, k, core).start()
    spread[...] = jnp.zeros_like(spread)
    for k in range(1, mems):
        core_copy(stats, stat_send, stat_recv, k, None).wait()
    everyone = members * mems
    for j in range(cells // chunk):
        at = slice(j * chunk, (j + 1) * chunk)

        def combined(base):
            sums = [stats[m, base : base + SUB, at] for m in range(mems)]
            mean = functools.reduce(jnp.add, sums) * (1.0 / everyone)
            total = functools.reduce(
                jnp.add, [stats[m, base + SUB : base + 2 * SUB, at] for m in range(mems)]
            )
            for s in sums:
                off = s * (1.0 / members) - mean
                total = total + members * (off * off)
            return mean, jnp.sqrt(total * (1.0 / (everyone - 1)) + variance_eps)

        prior_mean, prior_spread = combined(0)
        post_mean, post_spread = combined(2 * SUB)
        out_ref[0, :, at] = prior_mean
        out_ref[1, :, at] = 1.0 + relax_weight * (prior_spread - post_spread) / post_spread
        out_ref[2, :, at] = post_mean

    load_weight.wait()

    def wait_data(k, carry):
        data_copy(k, None).wait()
        return carry

    lax.fori_loop(1, tiles, wait_data, 0)
    picked = jnp.dot(pick[...], got[...], preferred_element_type=f32)
    count = count_ref[...]
    for p in range(pairs):
        live = lane < count[:, p : p + 1]
        for c in range(channels):
            value = jnp.zeros((rows, LANES), f32)
            for k in range(part):
                mine = picked[p * row_pad : p * row_pad + rows, k * LANES : (k + 1) * LANES]
                value = jnp.where((first + k == c) & (core * part < channels), mine, value)
            spread[p, pl.ds(c, rows, stride=SUB), :] = jnp.where(live, value, 0.0)
        spread[p, pl.ds(ONES, rows, stride=SUB), :] = jnp.where(live, 1.0, 0.0)

    group = next(n for n in (4, 3, 2, 1) if rows % n == 0)

    def remap(g, sums):
        for i in range(group):
            r = g * group + i
            here = pl.ds(pl.multiple_of(r * SUB, SUB), SUB)
            left = jnp.concatenate([spread[p, here, :] for p in range(pairs)], axis=1).astype(bf16)
            right = jnp.concatenate([weight[r, p] for p in range(pairs)], axis=1)
            product = lax.dot_general(
                left, right, (((1,), (1,)), ((), ())), preferred_element_type=f32
            )
            value = product / product[ONES : ONES + 1, :]
            coarse[core, :, pl.ds(pl.multiple_of(r * LANES, LANES), LANES)] = value
            sums = sums + value * area_ref[pl.ds(r, 1), :]
        return sums

    sums = lax.fori_loop(0, rows // group, remap, jnp.zeros((SUB, LANES), f32))

    for k in range(1, mems):
        core_copy(coarse, coarse_send, coarse_recv, k, core).start()
    eye = lax.broadcasted_iota(jnp.int32, (SUB, LANES), 0) == lax.broadcasted_iota(
        jnp.int32, (SUB, LANES), 1
    )
    total = jnp.sum(sums, axis=1, keepdims=True)
    level[pl.ds(flat, 1)] = jnp.sum(jnp.where(eye, total, 0.0), axis=0, keepdims=True)[None]

    def level_copy(k, here):
        other = lax.rem(flat + k, devices)
        source = here if here is not None else other
        return pltpu.make_async_remote_copy(
            src_ref=level.at[flat],
            dst_ref=level.at[source],
            send_sem=level_send.at[other],
            recv_sem=level_recv.at[source],
            device_id=(other // mems, lax.rem(other, mems)),
            device_id_type=MESH,
        )

    def start_level(k, carry):
        level_copy(k, flat).start()
        return carry

    def wait_level(k, carry):
        level_copy(k, None).wait()
        return carry

    lax.fori_loop(1, devices, start_level, 0)
    for k in range(1, mems):
        core_copy(coarse, coarse_send, coarse_recv, k, None).wait()
    lax.fori_loop(1, devices, wait_level, 0)
    row = level[0]
    for d in range(1, devices):
        row = row + level[d]
    weighted = jnp.sum(jnp.where(eye, row, 0.0), axis=1, keepdims=True)
    area = weighted[ONES : ONES + 1, :] * (1.0 / mems)
    mean = weighted / area
    for j in range(cells // chunk):
        at = slice(j * chunk, (j + 1) * chunk)
        value = functools.reduce(jnp.add, [coarse[m, :, at] for m in range(mems)])
        out_ref[0, :, at] = out_ref[0, :, at] + (value - mean)


def per_device(
    inc_fine, pair_owner, pair_block, pair_count, pair_weight, cell_area, prior, posterior
):
    tiles = lax.axis_size("tile")
    mems = lax.axis_size("mem")
    channels, fine_cells = inc_fine.shape
    rows, pairs = pair_owner.shape
    cells = prior.shape[2]
    fblocks = fine_cells // LANES
    cap = max(2, (2 * rows * pairs + tiles - 1) // tiles)
    cap = min(cap, rows)
    slots = round_up(cap, 16)
    part = -(-channels // mems)
    fine_pad = round_up(fblocks, LANES)
    row_pad = round_up(rows, 16)
    devices = tiles * mems
    vmem = pl.BlockSpec(memory_space=pltpu.VMEM)
    hbm = pl.BlockSpec(memory_space=pl.ANY)
    dma = pltpu.SemaphoreType.DMA
    small = pl.pallas_call(
        functools.partial(kernel, tiles, mems, cap),
        out_shape=jax.ShapeDtypeStruct((3, SUB, cells), f32),
        in_specs=[vmem] * 5 + [hbm] * 3,
        out_specs=vmem,
        scratch_shapes=[
            pltpu.VMEM(pair_weight.shape, bf16),
            pltpu.VMEM(prior.shape, bf16),
            pltpu.VMEM(posterior.shape, bf16),
            pltpu.VMEM((fblocks * SUB, LANES), f32),
            pltpu.VMEM((fine_pad, part * LANES), bf16),
            pltpu.VMEM((rows, LANES), f32),
            pltpu.VMEM((LANES, LANES), f32),
            pltpu.VMEM((tiles * slots, fine_pad), bf16),
            pltpu.VMEM((tiles, 1, LANES), f32),
            pltpu.VMEM((tiles, 1, LANES), f32),
            pltpu.VMEM((pairs * row_pad, tiles * slots), bf16),
            pltpu.VMEM((tiles * slots, part * LANES), bf16),
            pltpu.VMEM((tiles * slots, part * LANES), bf16),
            pltpu.VMEM((pairs, rows * SUB, LANES), f32),
            pltpu.VMEM((mems, 4 * SUB, cells), f32),
            pltpu.VMEM((mems, SUB, cells), f32),
            pltpu.VMEM((devices, 1, LANES), f32),
            dma((3,)),
            dma((tiles,)),
            dma((tiles,)),
            dma((tiles,)),
            dma((tiles,)),
            dma((mems,)),
            dma((mems,)),
            dma((mems,)),
            dma((mems,)),
            dma((devices,)),
            dma((devices,)),
        ],
        compiler_params=pltpu.CompilerParams(
            collective_id=0, has_side_effects=True, vmem_limit_bytes=48 * 1024 * 1024
        ),
        name="remap_and_spread",
    )(
        inc_fine,
        pair_owner,
        pair_block,
        pair_count,
        cell_area.reshape(rows, -1),
        pair_weight,
        prior,
        posterior,
    )
    center, factor, post_mean = (small[i, :channels, None, :] for i in range(3))
    return (center + factor * (posterior.astype(f32) - post_mean)).astype(bf16)


def solution(mesh):
    in_specs = (
        P(None, "tile"),
        P("tile", None),
        P("tile", None),
        P("tile", None),
        P("tile", None, None, None),
        P("tile"),
        P(None, "mem", "tile"),
        P(None, "mem", "tile"),
    )
    out_specs = P(None, "mem", "tile")
    return jax.shard_map(
        per_device, mesh=mesh, in_specs=in_specs, out_specs=out_specs, check_vma=False
    )
```

```python
import functools

import jax
import jax.numpy as jnp
from jax import lax
from jax.experimental import pallas as pl
from jax.experimental.pallas import tpu as pltpu
from jax.sharding import PartitionSpec as P

relax_weight = 0.85
variance_eps = 1e-06
f32 = jnp.float32
bf16 = jnp.bfloat16
MESH = pl.DeviceIdType.MESH
LANES = 128
SUB = 8
ONES = 7


def round_up(n, k):
    return -(-n // k) * k


def kernel(
    tiles,
    mems,
    cap,
    inc_hbm,
    owner_hbm,
    block_hbm,
    count_hbm,
    area_hbm,
    weight_hbm,
    prior_hbm,
    post_hbm,
    out_ref,
    inc_ref,
    index,
    area_ref,
    weight,
    prior,
    post,
    tall,
    fine,
    before,
    square,
    hits,
    ask,
    asked,
    pick,
    served,
    got,
    spread,
    stats,
    coarse,
    level,
    local_sem,
    ask_send,
    ask_recv,
    data_send,
    data_recv,
    stat_send,
    stat_recv,
    coarse_send,
    coarse_recv,
    level_send,
    level_recv,
):
    channels = inc_ref.shape[0]
    pairs, rows = owner_hbm.shape
    fblocks = inc_ref.shape[1] // LANES
    fine_pad = fine.shape[0]
    part = got.shape[1] // LANES
    slots = got.shape[0] // tiles
    row_pad = pick.shape[0] // pairs
    members, cells = prior.shape[1], prior.shape[2]
    devices = tiles * mems
    me = lax.axis_index("tile")
    core = lax.axis_index("mem")
    flat = me * mems + core
    first = jnp.minimum(core * part, channels - part)

    loads = [
        pltpu.make_async_copy(source, target, local_sem.at[i])
        for i, (source, target) in enumerate(
            [
                (owner_hbm, index.at[0]),
                (block_hbm, index.at[1]),
                (count_hbm, index.at[2]),
                (inc_hbm, inc_ref),
                (prior_hbm, prior),
                (weight_hbm, weight),
                (post_hbm, post),
                (area_hbm, area_ref),
            ]
        )
    ]
    for load in loads[:4]:
        load.start()

    barrier = pltpu.get_barrier_semaphore()

    def greet(k, carry):
        other = lax.rem(flat + k, devices)
        pl.semaphore_signal(
            barrier, inc=1, device_id=(other // mems, lax.rem(other, mems)), device_id_type=MESH
        )
        return carry

    lax.fori_loop(1, devices, greet, 0)
    for load in loads[4:]:
        load.start()

    lane = lax.broadcasted_iota(jnp.int32, (rows, LANES), 1).astype(f32)
    square[...] = jnp.zeros_like(square)
    for load in loads[:3]:
        load.wait()
    for i in range(3):
        square[i * SUB : i * SUB + pairs, :rows] = index[i].astype(f32)
    turned = jnp.transpose(square[...])[:rows]
    owner, block, count = (turned[:, i * SUB : i * SUB + pairs] for i in range(3))
    named = [owner[:, p : p + 1] == lane for p in range(pairs)]
    any_named = jnp.zeros((rows, LANES), f32)
    wanted = jnp.zeros((rows, LANES), f32)
    for p in range(pairs):
        any_named = any_named + jnp.where(named[p], 1.0, 0.0)
        wanted = wanted + jnp.where(named[p], block[:, p : p + 1] + 1.0, 0.0)
    run = jnp.zeros((1, LANES), f32)
    for r in range(rows):
        before[r : r + 1, :] = run
        run = run + any_named[r : r + 1, :]
    earlier = before[...]
    square[...] = jnp.zeros_like(square)
    for s in range(cap):
        chosen = jnp.where((earlier == float(s)) & (any_named > 0.0), wanted, 0.0)
        square[s : s + 1, :] = jnp.sum(chosen, axis=0, keepdims=True)
    turned = jnp.transpose(square[...]) - 1.0
    for t in range(tiles):
        ask[t] = turned[t : t + 1, :]

    loads[3].wait()
    for b in range(fblocks):
        tall[b * SUB : b * SUB + channels, :] = inc_ref[:, b * LANES : (b + 1) * LANES].astype(f32)
    fine[...] = jnp.zeros_like(fine)
    planes = [tall[pl.ds(c, fblocks, stride=SUB), :] for c in range(channels)]
    for k in range(part):
        value = planes[k]
        for c in range(1, channels):
            value = jnp.where(first + k == c, planes[c], value)
        fine[:fblocks, k * LANES : (k + 1) * LANES] = value.astype(bf16)

    wide = lax.broadcasted_iota(jnp.int32, (rows, tiles * slots), 1).astype(f32)
    pick[...] = jnp.zeros_like(pick)
    for p in range(pairs):
        slot = jnp.sum(jnp.where(named[p], earlier, 0.0), axis=1, keepdims=True)
        place = owner[:, p : p + 1] * float(slots) + slot
        pick[p * row_pad : p * row_pad + rows, :] = jnp.where(wide == place, 1.0, 0.0).astype(bf16)

    live = [lane < count[:, p : p + 1] for p in range(pairs)]
    spread[...] = jnp.zeros_like(spread)
    for p in range(pairs):
        spread[p, pl.ds(ONES, rows, stride=SUB), :] = jnp.where(live[p], 1.0, 0.0)

    pl.semaphore_wait(barrier, devices - 1)

    def start_ask(k, carry):
        other = lax.rem(me + k, tiles)
        pltpu.make_async_remote_copy(
            src_ref=ask.at[other],
            dst_ref=asked.at[me],
            send_sem=ask_send,
            recv_sem=ask_recv,
            device_id=(other, core),
            device_id_type=MESH,
        ).start()
        return carry

    lax.fori_loop(1, tiles, start_ask, 0)
    asked[pl.ds(me, 1)] = ask[pl.ds(me, 1)]

    chunk = next(n for n in (512, 384, 256, 128) if cells % n == 0)
    sub = lax.broadcasted_iota(jnp.int32, (SUB, chunk), 0)

    def member_stats(ref, base):
        def body(j, carry):
            at = pl.ds(pl.multiple_of(j * chunk, chunk), chunk)
            sums = jnp.zeros((SUB, chunk), f32)
            squares = jnp.zeros((SUB, chunk), f32)
            for c in range(channels):
                values = ref[c, :, at].astype(f32)
                total = jnp.sum(values, axis=0, keepdims=True)
                dev = values - total * (1.0 / members)
                sq = jnp.sum(dev * dev, axis=0, keepdims=True)
                sums = jnp.where(sub == c, total, sums)
                squares = jnp.where(sub == c, sq, squares)
            stats[core, base : base + SUB, at] = sums
            stats[core, base + SUB : base + 2 * SUB, at] = squares
            return carry

        lax.fori_loop(0, cells // chunk, body, 0)

    loads[4].wait()
    member_stats(prior, 0)

    def wait_all(buffer, sem):
        pltpu.make_async_copy(buffer, buffer, sem).wait()

    wait_all(asked.at[: tiles - 1], ask_recv)
    square[...] = jnp.zeros_like(square)
    for t in range(tiles):
        square[t : t + 1, :] = asked[t]
    turned = jnp.transpose(square[...])
    fine_lane = lax.broadcasted_iota(jnp.int32, (slots, fine_pad), 1).astype(f32)
    for t in range(tiles):
        hits[t * slots : (t + 1) * slots, :] = jnp.where(
            turned[:slots, t : t + 1] == fine_lane, 1.0, 0.0
        ).astype(bf16)
    served[...] = jnp.dot(hits[...], fine[...], preferred_element_type=f32).astype(bf16)

    def rows_of(t):
        return pl.ds(pl.multiple_of(t * slots, slots), slots)

    def start_data(k, carry):
        other = lax.rem(me + k, tiles)
        pltpu.make_async_remote_copy(
            src_ref=served.at[rows_of(other)],
            dst_ref=got.at[rows_of(me)],
            send_sem=data_send,
            recv_sem=data_recv,
            device_id=(other, core),
            device_id_type=MESH,
        ).start()
        return carry

    lax.fori_loop(1, tiles, start_data, 0)
    got[rows_of(me), :] = served[rows_of(me), :]

    loads[6].wait()
    member_stats(post, 2 * SUB)

    def core_copy(buffer, send, recv, k, here):
        other = lax.rem(core + k, mems)
        source = here if here is not None else other
        return pltpu.make_async_remote_copy(
            src_ref=buffer.at[core],
            dst_ref=buffer.at[source],
            send_sem=send.at[other],
            recv_sem=recv.at[source],
            device_id=(me, other),
            device_id_type=MESH,
        )

    for k in range(1, mems):
        core_copy(stats, stat_send, stat_recv, k, core).start()
    for k in range(1, mems):
        core_copy(stats, stat_send, stat_recv, k, None).wait()
    everyone = members * mems
    for j in range(cells // chunk):
        at = slice(j * chunk, (j + 1) * chunk)

        def combined(base):
            sums = [stats[m, base : base + SUB, at] for m in range(mems)]
            mean = functools.reduce(jnp.add, sums) * (1.0 / everyone)
            total = functools.reduce(
                jnp.add, [stats[m, base + SUB : base + 2 * SUB, at] for m in range(mems)]
            )
            for s in sums:
                off = s * (1.0 / members) - mean
                total = total + members * (off * off)
            return mean, jnp.sqrt(total * (1.0 / (everyone - 1)) + variance_eps)

        prior_mean, prior_spread = combined(0)
        post_mean, post_spread = combined(2 * SUB)
        out_ref[0, :, at] = prior_mean
        out_ref[1, :, at] = 1.0 + relax_weight * (prior_spread - post_spread) / post_spread
        out_ref[2, :, at] = post_mean

    loads[5].wait()
    loads[7].wait()

    wait_all(got.at[: (tiles - 1) * slots], data_recv)
    picked = jnp.dot(pick[...], got[...], preferred_element_type=f32)
    for p in range(pairs):
        for c in range(channels):
            value = jnp.zeros((rows, LANES), f32)
            for k in range(part):
                mine = picked[p * row_pad : p * row_pad + rows, k * LANES : (k + 1) * LANES]
                value = jnp.where((first + k == c) & (core * part < channels), mine, value)
            spread[p, pl.ds(c, rows, stride=SUB), :] = jnp.where(live[p], value, 0.0)

    group = next(n for n in (12, 8, 4, 3, 2, 1) if rows % n == 0)

    def remap(g, sums):
        for i in range(group):
            r = g * group + i
            here = pl.ds(pl.multiple_of(r * SUB, SUB), SUB)
            left = jnp.concatenate([spread[p, here, :] for p in range(pairs)], axis=1).astype(bf16)
            right = jnp.concatenate([weight[r, p] for p in range(pairs)], axis=1)
            product = lax.dot_general(
                left, right, (((1,), (1,)), ((), ())), preferred_element_type=f32
            )
            value = product / product[ONES : ONES + 1, :]
            coarse[core, :, pl.ds(pl.multiple_of(r * LANES, LANES), LANES)] = value
            sums = sums + value * area_ref[pl.ds(r, 1), :]
        return sums

    sums = lax.fori_loop(0, rows // group, remap, jnp.zeros((SUB, LANES), f32))

    for k in range(1, mems):
        core_copy(coarse, coarse_send, coarse_recv, k, core).start()
    eye = lax.broadcasted_iota(jnp.int32, (SUB, LANES), 0) == lax.broadcasted_iota(
        jnp.int32, (SUB, LANES), 1
    )
    total = jnp.sum(sums, axis=1, keepdims=True)
    level[pl.ds(flat, 1)] = jnp.sum(jnp.where(eye, total, 0.0), axis=0, keepdims=True)[None]

    def start_level(k, carry):
        other = lax.rem(flat + k, devices)
        pltpu.make_async_remote_copy(
            src_ref=level.at[flat],
            dst_ref=level.at[flat],
            send_sem=level_send,
            recv_sem=level_recv,
            device_id=(other // mems, lax.rem(other, mems)),
            device_id_type=MESH,
        ).start()
        return carry

    lax.fori_loop(1, devices, start_level, 0)
    for k in range(1, mems):
        core_copy(coarse, coarse_send, coarse_recv, k, None).wait()
    wait_all(level.at[: devices - 1], level_recv)
    row = level[0]
    for d in range(1, devices):
        row = row + level[d]
    weighted = jnp.sum(jnp.where(eye, row, 0.0), axis=1, keepdims=True)
    area = weighted[ONES : ONES + 1, :] * (1.0 / mems)
    mean = weighted / area
    for j in range(cells // chunk):
        at = slice(j * chunk, (j + 1) * chunk)
        value = functools.reduce(jnp.add, [coarse[m, :, at] for m in range(mems)])
        out_ref[0, :, at] = out_ref[0, :, at] + (value - mean)
    wait_all(asked.at[: tiles - 1], ask_send)
    wait_all(got.at[: (tiles - 1) * slots], data_send)
    wait_all(level.at[: devices - 1], level_send)


def per_device(
    inc_fine, pair_owner, pair_block, pair_count, pair_weight, cell_area, prior, posterior
):
    tiles = lax.axis_size("tile")
    mems = lax.axis_size("mem")
    channels, fine_cells = inc_fine.shape
    rows, pairs = pair_owner.shape
    cells = prior.shape[2]
    fblocks = fine_cells // LANES
    cap = max(2, (2 * rows * pairs + tiles - 1) // tiles)
    cap = min(cap, rows)
    slots = round_up(cap, 16)
    part = -(-channels // mems)
    fine_pad = round_up(fblocks, LANES)
    row_pad = round_up(rows, 16)
    devices = tiles * mems
    vmem = pl.BlockSpec(memory_space=pltpu.VMEM)
    hbm = pl.BlockSpec(memory_space=pltpu.HBM)
    dma = pltpu.SemaphoreType.DMA
    small = pl.pallas_call(
        functools.partial(kernel, tiles, mems, cap),
        out_shape=pltpu.VMEM((3, SUB, cells), f32),
        in_specs=[hbm] * 8,
        out_specs=vmem,
        scratch_shapes=[
            pltpu.VMEM(inc_fine.shape, bf16),
            pltpu.VMEM((3, pairs, rows), jnp.int32),
            pltpu.VMEM((rows, LANES), f32),
            pltpu.VMEM(pair_weight.shape, bf16),
            pltpu.VMEM(prior.shape, bf16),
            pltpu.VMEM(posterior.shape, bf16),
            pltpu.VMEM((fblocks * SUB, LANES), f32),
            pltpu.VMEM((fine_pad, part * LANES), bf16),
            pltpu.VMEM((rows, LANES), f32),
            pltpu.VMEM((LANES, LANES), f32),
            pltpu.VMEM((tiles * slots, fine_pad), bf16),
            pltpu.VMEM((tiles, 1, LANES), f32),
            pltpu.VMEM((tiles, 1, LANES), f32),
            pltpu.VMEM((pairs * row_pad, tiles * slots), bf16),
            pltpu.VMEM((tiles * slots, part * LANES), bf16),
            pltpu.VMEM((tiles * slots, part * LANES), bf16),
            pltpu.VMEM((pairs, rows * SUB, LANES), f32),
            pltpu.VMEM((mems, 4 * SUB, cells), f32),
            pltpu.VMEM((mems, SUB, cells), f32),
            pltpu.VMEM((devices, 1, LANES), f32),
            dma((8,)),
            dma,
            dma,
            dma,
            dma,
            dma((mems,)),
            dma((mems,)),
            dma((mems,)),
            dma((mems,)),
            dma,
            dma,
        ],
        compiler_params=pltpu.CompilerParams(
            collective_id=0, has_side_effects=True, vmem_limit_bytes=56 * 1024 * 1024
        ),
        name="remap_and_spread",
    )(
        inc_fine,
        pair_owner.T,
        pair_block.T,
        pair_count.T,
        cell_area.reshape(rows, -1),
        pair_weight,
        prior,
        posterior,
    )
    center, factor, post_mean = (small[i, :channels, None, :] for i in range(3))
    return (center + factor * (posterior.astype(f32) - post_mean)).astype(bf16)


def solution(mesh):
    in_specs = (
        P(None, "tile"),
        P("tile", None),
        P("tile", None),
        P("tile", None),
        P("tile", None, None, None),
        P("tile"),
        P(None, "mem", "tile"),
        P(None, "mem", "tile"),
    )
    out_specs = P(None, "mem", "tile")
    return jax.shard_map(
        per_device, mesh=mesh, in_specs=in_specs, out_specs=out_specs, check_vma=False
    )
```

```python
import functools

import jax
import jax.numpy as jnp
from jax import lax
from jax.experimental import pallas as pl
from jax.experimental.pallas import tpu as pltpu
from jax.sharding import PartitionSpec as P

relax_weight = 0.85
variance_eps = 1e-06
f32 = jnp.float32
bf16 = jnp.bfloat16
MESH = pl.DeviceIdType.MESH
LANES = 128
SUB = 8
ONES = 7


def round_up(n, k):
    return -(-n // k) * k


def kernel(
    tiles,
    mems,
    cap,
    inc_hbm,
    owner_hbm,
    block_hbm,
    count_hbm,
    area_hbm,
    weight_hbm,
    prior_hbm,
    post_hbm,
    out_ref,
    inc_ref,
    index,
    area_ref,
    weight,
    prior,
    post,
    tall,
    fine,
    before,
    square,
    hits,
    ask,
    asked,
    pick,
    served,
    got,
    spread,
    stats,
    coarse,
    level,
    local_sem,
    ask_send,
    ask_recv,
    data_send,
    data_recv,
    stat_send,
    stat_recv,
    coarse_send,
    coarse_recv,
    level_send,
    level_recv,
):
    channels = inc_ref.shape[0]
    pairs, rows = owner_hbm.shape
    fblocks = inc_ref.shape[1] // LANES
    fine_pad = fine.shape[0]
    part = got.shape[1] // LANES
    slots = got.shape[0] // tiles
    row_pad = pick.shape[0] // pairs
    members, cells = prior.shape[1], prior.shape[2]
    devices = tiles * mems
    me = lax.axis_index("tile")
    core = lax.axis_index("mem")
    flat = me * mems + core
    first = jnp.minimum(core * part, channels - part)

    def wrap(n, size):
        return jnp.where(n >= size, n - size, n)

    def for_all(size, action):
        def body(k, carry):
            action(k)
            return carry

        lax.fori_loop(1, size, body, 0)

    def for_devices(action):
        for m in range(mems):
            for_all(tiles, lambda k: action(wrap(me + k, tiles), m))
            if m > 0:
                action(me, wrap(core + m, mems))

    loads = [
        pltpu.make_async_copy(source, target, local_sem.at[i])
        for i, (source, target) in enumerate(
            [
                (owner_hbm, index.at[0]),
                (block_hbm, index.at[1]),
                (count_hbm, index.at[2]),
                (inc_hbm, inc_ref),
                (prior_hbm, prior),
                (weight_hbm, weight),
                (post_hbm, post),
                (area_hbm, area_ref),
            ]
        )
    ]
    for load in loads[:4]:
        load.start()

    barrier = pltpu.get_barrier_semaphore()

    def greet(tile, mem):
        pl.semaphore_signal(barrier, inc=1, device_id=(tile, mem), device_id_type=MESH)

    for_devices(greet)
    for load in loads[4:]:
        load.start()

    lane = lax.broadcasted_iota(jnp.int32, (rows, LANES), 1).astype(f32)
    square[...] = jnp.zeros_like(square)
    for load in loads[:3]:
        load.wait()
    for i in range(3):
        square[i * SUB : i * SUB + pairs, :rows] = index[i].astype(f32)
    turned = jnp.transpose(square[...])[:rows]
    owner, block, count = (turned[:, i * SUB : i * SUB + pairs] for i in range(3))
    named = [owner[:, p : p + 1] == lane for p in range(pairs)]
    any_named = jnp.zeros((rows, LANES), f32)
    wanted = jnp.zeros((rows, LANES), f32)
    for p in range(pairs):
        any_named = any_named + jnp.where(named[p], 1.0, 0.0)
        wanted = wanted + jnp.where(named[p], block[:, p : p + 1] + 1.0, 0.0)
    run = jnp.zeros((1, LANES), f32)
    for r in range(rows):
        before[r : r + 1, :] = run
        run = run + any_named[r : r + 1, :]
    earlier = before[...]
    square[...] = jnp.zeros_like(square)
    for s in range(cap):
        chosen = jnp.where((earlier == float(s)) & (any_named > 0.0), wanted, 0.0)
        square[s : s + 1, :] = jnp.sum(chosen, axis=0, keepdims=True)
    turned = jnp.transpose(square[...]) - 1.0
    for t in range(tiles):
        ask[t] = turned[t : t + 1, :]

    pl.semaphore_wait(barrier, devices - 1)

    def start_ask(k):
        other = wrap(me + k, tiles)
        pltpu.make_async_remote_copy(
            src_ref=ask.at[other],
            dst_ref=asked.at[me],
            send_sem=ask_send,
            recv_sem=ask_recv,
            device_id=(other, core),
            device_id_type=MESH,
        ).start()

    for_all(tiles, start_ask)
    asked[pl.ds(me, 1)] = ask[pl.ds(me, 1)]

    loads[3].wait()
    for b in range(fblocks):
        tall[b * SUB : b * SUB + channels, :] = inc_ref[:, b * LANES : (b + 1) * LANES].astype(f32)
    fine[...] = jnp.zeros_like(fine)
    planes = [tall[pl.ds(c, fblocks, stride=SUB), :] for c in range(channels)]
    for k in range(part):
        value = planes[k]
        for c in range(1, channels):
            value = jnp.where(first + k == c, planes[c], value)
        fine[:fblocks, k * LANES : (k + 1) * LANES] = value.astype(bf16)

    wide = lax.broadcasted_iota(jnp.int32, (rows, tiles * slots), 1).astype(f32)
    pick[...] = jnp.zeros_like(pick)
    for p in range(pairs):
        slot = jnp.sum(jnp.where(named[p], earlier, 0.0), axis=1, keepdims=True)
        place = owner[:, p : p + 1] * float(slots) + slot
        pick[p * row_pad : p * row_pad + rows, :] = jnp.where(wide == place, 1.0, 0.0).astype(bf16)

    live = [lane < count[:, p : p + 1] for p in range(pairs)]
    spread[...] = jnp.zeros_like(spread)
    for p in range(pairs):
        spread[p, pl.ds(ONES, rows, stride=SUB), :] = jnp.where(live[p], 1.0, 0.0)

    chunk = next(n for n in (512, 384, 256, 128) if cells % n == 0)
    sub = lax.broadcasted_iota(jnp.int32, (SUB, chunk), 0)

    def member_stats(ref, base):
        def body(j, carry):
            at = pl.ds(pl.multiple_of(j * chunk, chunk), chunk)
            sums = jnp.zeros((SUB, chunk), f32)
            squares = jnp.zeros((SUB, chunk), f32)
            for c in range(channels):
                values = ref[c, :, at].astype(f32)
                total = jnp.sum(values, axis=0, keepdims=True)
                dev = values - total * (1.0 / members)
                sq = jnp.sum(dev * dev, axis=0, keepdims=True)
                sums = jnp.where(sub == c, total, sums)
                squares = jnp.where(sub == c, sq, squares)
            stats[core, base : base + SUB, at] = sums
            stats[core, base + SUB : base + 2 * SUB, at] = squares
            return carry

        lax.fori_loop(0, cells // chunk, body, 0)

    def wait_all(buffer, sem):
        pltpu.make_async_copy(buffer, buffer, sem).wait()

    wait_all(asked.at[: tiles - 1], ask_recv)
    square[...] = jnp.zeros_like(square)
    for t in range(tiles):
        square[t : t + 1, :] = asked[t]
    turned = jnp.transpose(square[...])
    fine_lane = lax.broadcasted_iota(jnp.int32, (slots, fine_pad), 1).astype(f32)
    for t in range(tiles):
        hits[t * slots : (t + 1) * slots, :] = jnp.where(
            turned[:slots, t : t + 1] == fine_lane, 1.0, 0.0
        ).astype(bf16)
    served[...] = jnp.dot(hits[...], fine[...], preferred_element_type=f32).astype(bf16)

    def rows_of(t):
        return pl.ds(pl.multiple_of(t * slots, slots), slots)

    def start_data(k):
        other = wrap(me + wrap(k - 1 + tiles // 2, tiles - 1) + 1, tiles)
        pltpu.make_async_remote_copy(
            src_ref=served.at[rows_of(other)],
            dst_ref=got.at[rows_of(me)],
            send_sem=data_send,
            recv_sem=data_recv,
            device_id=(other, core),
            device_id_type=MESH,
        ).start()

    for_all(tiles, start_data)
    got[rows_of(me), :] = served[rows_of(me), :]

    loads[4].wait()
    member_stats(prior, 0)
    loads[6].wait()
    member_stats(post, 2 * SUB)

    def core_copy(buffer, send, recv, k, here):
        other = wrap(core + k, mems)
        source = here if here is not None else other
        return pltpu.make_async_remote_copy(
            src_ref=buffer.at[core],
            dst_ref=buffer.at[source],
            send_sem=send.at[other],
            recv_sem=recv.at[source],
            device_id=(me, other),
            device_id_type=MESH,
        )

    for k in range(1, mems):
        core_copy(stats, stat_send, stat_recv, k, core).start()
    for k in range(1, mems):
        core_copy(stats, stat_send, stat_recv, k, None).wait()
    everyone = members * mems
    for j in range(cells // chunk):
        at = slice(j * chunk, (j + 1) * chunk)

        def combined(base):
            sums = [stats[m, base : base + SUB, at] for m in range(mems)]
            mean = functools.reduce(jnp.add, sums) * (1.0 / everyone)
            total = functools.reduce(
                jnp.add, [stats[m, base + SUB : base + 2 * SUB, at] for m in range(mems)]
            )
            for s in sums:
                off = s * (1.0 / members) - mean
                total = total + members * (off * off)
            return mean, jnp.sqrt(total * (1.0 / (everyone - 1)) + variance_eps)

        prior_mean, prior_spread = combined(0)
        post_mean, post_spread = combined(2 * SUB)
        out_ref[0, :, at] = prior_mean
        out_ref[1, :, at] = 1.0 + relax_weight * (prior_spread - post_spread) / post_spread
        out_ref[2, :, at] = post_mean

    loads[5].wait()
    loads[7].wait()

    wait_all(got.at[: (tiles - 1) * slots], data_recv)
    picked = jnp.dot(pick[...], got[...], preferred_element_type=f32)
    for p in range(pairs):
        for c in range(channels):
            value = jnp.zeros((rows, LANES), f32)
            for k in range(part):
                mine = picked[p * row_pad : p * row_pad + rows, k * LANES : (k + 1) * LANES]
                value = jnp.where((first + k == c) & (core * part < channels), mine, value)
            spread[p, pl.ds(c, rows, stride=SUB), :] = jnp.where(live[p], value, 0.0)

    sums = jnp.zeros((SUB, LANES), f32)
    for r in range(rows):
        left = jnp.concatenate(
            [spread[p, r * SUB : (r + 1) * SUB, :] for p in range(pairs)], axis=1
        ).astype(bf16)
        right = jnp.concatenate([weight[r, p] for p in range(pairs)], axis=1)
        product = lax.dot_general(
            left, right, (((1,), (1,)), ((), ())), preferred_element_type=f32
        )
        value = product / product[ONES : ONES + 1, :]
        coarse[core, :, r * LANES : (r + 1) * LANES] = value
        sums = sums + value * area_ref[r : r + 1, :]

    for k in range(1, mems):
        core_copy(coarse, coarse_send, coarse_recv, k, core).start()
    eye = lax.broadcasted_iota(jnp.int32, (SUB, LANES), 0) == lax.broadcasted_iota(
        jnp.int32, (SUB, LANES), 1
    )
    total = jnp.sum(sums, axis=1, keepdims=True)
    level[pl.ds(flat, 1)] = jnp.sum(jnp.where(eye, total, 0.0), axis=0, keepdims=True)[None]

    def start_level(tile, mem):
        pltpu.make_async_remote_copy(
            src_ref=level.at[flat],
            dst_ref=level.at[flat],
            send_sem=level_send,
            recv_sem=level_recv,
            device_id=(tile, mem),
            device_id_type=MESH,
        ).start()

    for_devices(start_level)
    for k in range(1, mems):
        core_copy(coarse, coarse_send, coarse_recv, k, None).wait()
    wait_all(level.at[: devices - 1], level_recv)
    row = level[0]
    for d in range(1, devices):
        row = row + level[d]
    weighted = jnp.sum(jnp.where(eye, row, 0.0), axis=1, keepdims=True)
    area = weighted[ONES : ONES + 1, :] * (1.0 / mems)
    mean = weighted / area
    for j in range(cells // chunk):
        at = slice(j * chunk, (j + 1) * chunk)
        value = functools.reduce(jnp.add, [coarse[m, :, at] for m in range(mems)])
        out_ref[0, :, at] = out_ref[0, :, at] + (value - mean)
    wait_all(asked.at[: tiles - 1], ask_send)
    wait_all(got.at[: (tiles - 1) * slots], data_send)
    wait_all(level.at[: devices - 1], level_send)


def per_device(
    inc_fine, pair_owner, pair_block, pair_count, pair_weight, cell_area, prior, posterior
):
    tiles = lax.axis_size("tile")
    mems = lax.axis_size("mem")
    channels, fine_cells = inc_fine.shape
    rows, pairs = pair_owner.shape
    cells = prior.shape[2]
    fblocks = fine_cells // LANES
    cap = max(2, (2 * rows * pairs + tiles - 1) // tiles)
    cap = min(cap, rows)
    slots = round_up(cap, 16)
    part = -(-channels // mems)
    fine_pad = round_up(fblocks, LANES)
    row_pad = round_up(rows, 16)
    devices = tiles * mems
    vmem = pl.BlockSpec(memory_space=pltpu.VMEM)
    hbm = pl.BlockSpec(memory_space=pltpu.HBM)
    dma = pltpu.SemaphoreType.DMA
    small = pl.pallas_call(
        functools.partial(kernel, tiles, mems, cap),
        out_shape=pltpu.VMEM((3, SUB, cells), f32),
        in_specs=[hbm] * 8,
        out_specs=vmem,
        scratch_shapes=[
            pltpu.VMEM(inc_fine.shape, bf16),
            pltpu.VMEM((3, pairs, rows), jnp.int32),
            pltpu.VMEM((rows, LANES), f32),
            pltpu.VMEM(pair_weight.shape, bf16),
            pltpu.VMEM(prior.shape, bf16),
            pltpu.VMEM(posterior.shape, bf16),
            pltpu.VMEM((fblocks * SUB, LANES), f32),
            pltpu.VMEM((fine_pad, part * LANES), bf16),
            pltpu.VMEM((rows, LANES), f32),
            pltpu.VMEM((LANES, LANES), f32),
            pltpu.VMEM((tiles * slots, fine_pad), bf16),
            pltpu.VMEM((tiles, 1, LANES), f32),
            pltpu.VMEM((tiles, 1, LANES), f32),
            pltpu.VMEM((pairs * row_pad, tiles * slots), bf16),
            pltpu.VMEM((tiles * slots, part * LANES), bf16),
            pltpu.VMEM((tiles * slots, part * LANES), bf16),
            pltpu.VMEM((pairs, rows * SUB, LANES), f32),
            pltpu.VMEM((mems, 4 * SUB, cells), f32),
            pltpu.VMEM((mems, SUB, cells), f32),
            pltpu.VMEM((devices, 1, LANES), f32),
            dma((8,)),
            dma,
            dma,
            dma,
            dma,
            dma((mems,)),
            dma((mems,)),
            dma((mems,)),
            dma((mems,)),
            dma,
            dma,
        ],
        compiler_params=pltpu.CompilerParams(
            collective_id=0, has_side_effects=True, vmem_limit_bytes=56 * 1024 * 1024
        ),
        name="remap_and_spread",
    )(
        inc_fine,
        pair_owner.T,
        pair_block.T,
        pair_count.T,
        cell_area.reshape(rows, -1),
        pair_weight,
        prior,
        posterior,
    )
    center, factor, post_mean = (small[i, :channels, None, :] for i in range(3))
    return (center + factor * (posterior.astype(f32) - post_mean)).astype(bf16)


def solution(mesh):
    in_specs = (
        P(None, "tile"),
        P("tile", None),
        P("tile", None),
        P("tile", None),
        P("tile", None, None, None),
        P("tile"),
        P(None, "mem", "tile"),
        P(None, "mem", "tile"),
    )
    out_specs = P(None, "mem", "tile")
    return jax.shard_map(
        per_device, mesh=mesh, in_specs=in_specs, out_specs=out_specs, check_vma=False
    )
```

```python
import functools

import jax
import jax.numpy as jnp
from jax import lax
from jax.experimental import pallas as pl
from jax.experimental.pallas import tpu as pltpu
from jax.sharding import PartitionSpec as P

relax_weight = 0.85
variance_eps = 1e-06
f32 = jnp.float32
bf16 = jnp.bfloat16
MESH = pl.DeviceIdType.MESH
LANES = 128
SUB = 8
ONES = 7


def round_up(n, k):
    return -(-n // k) * k


def kernel(
    tiles,
    mems,
    cap,
    inc_hbm,
    owner_hbm,
    block_hbm,
    count_hbm,
    area_hbm,
    weight_hbm,
    prior_hbm,
    post_hbm,
    out_ref,
    inc_ref,
    index,
    area_ref,
    weight,
    prior,
    post,
    tall,
    fine,
    before,
    square,
    hits,
    ask,
    asked,
    pick,
    served,
    got,
    spread,
    ratio,
    shares,
    stats,
    coarse,
    level,
    local_sem,
    ask_send,
    ask_recv,
    data_send,
    data_recv,
    stat_send,
    stat_recv,
    coarse_send,
    coarse_recv,
    level_send,
    level_recv,
):
    channels = inc_ref.shape[0]
    pairs, rows = owner_hbm.shape
    fblocks = inc_ref.shape[1] // LANES
    fine_pad = fine.shape[0]
    part = got.shape[1] // LANES
    slots = got.shape[0] // tiles
    row_pad = pick.shape[0] // pairs
    members, cells = prior.shape[1], prior.shape[2]
    devices = tiles * mems
    me = lax.axis_index("tile")
    core = lax.axis_index("mem")
    flat = me * mems + core
    first = jnp.minimum(core * part, channels - part)

    def wrap(n, size):
        return jnp.where(n >= size, n - size, n)

    def for_all(size, action):
        def body(k, carry):
            action(k)
            return carry

        lax.fori_loop(1, size, body, 0)

    def for_devices(action):
        for m in range(mems):
            for_all(tiles, lambda k: action(wrap(me + k, tiles), m))
            if m > 0:
                action(me, wrap(core + m, mems))

    loads = [
        pltpu.make_async_copy(source, target, local_sem.at[i])
        for i, (source, target) in enumerate(
            [
                (owner_hbm, index.at[0]),
                (block_hbm, index.at[1]),
                (count_hbm, index.at[2]),
                (inc_hbm, inc_ref),
                (prior_hbm, prior),
                (weight_hbm, weight),
                (post_hbm, post),
                (area_hbm, area_ref),
            ]
        )
    ]
    for load in loads[:4]:
        load.start()

    barrier = pltpu.get_barrier_semaphore()

    def greet(tile, mem):
        pl.semaphore_signal(barrier, inc=1, device_id=(tile, mem), device_id_type=MESH)

    for_devices(greet)
    for load in loads[4:]:
        load.start()

    lane = lax.broadcasted_iota(jnp.int32, (rows, LANES), 1).astype(f32)
    square[...] = jnp.zeros_like(square)
    for load in loads[:3]:
        load.wait()
    for i in range(3):
        square[i * SUB : i * SUB + pairs, :rows] = index[i].astype(f32)
    turned = jnp.transpose(square[...])[:rows]
    owner, block, count = (turned[:, i * SUB : i * SUB + pairs] for i in range(3))
    named = [owner[:, p : p + 1] == lane for p in range(pairs)]
    any_named = jnp.zeros((rows, LANES), f32)
    wanted = jnp.zeros((rows, LANES), f32)
    for p in range(pairs):
        any_named = any_named + jnp.where(named[p], 1.0, 0.0)
        wanted = wanted + jnp.where(named[p], block[:, p : p + 1] + 1.0, 0.0)
    run = jnp.zeros((1, LANES), f32)
    for r in range(rows):
        before[r : r + 1, :] = run
        run = run + any_named[r : r + 1, :]
    earlier = before[...]
    square[...] = jnp.zeros_like(square)
    for s in range(cap):
        chosen = jnp.where((earlier == float(s)) & (any_named > 0.0), wanted, 0.0)
        square[s : s + 1, :] = jnp.sum(chosen, axis=0, keepdims=True)
    turned = jnp.transpose(square[...]) - 1.0
    for t in range(tiles):
        ask[t] = turned[t : t + 1, :]

    pl.semaphore_wait(barrier, devices - 1)

    def start_ask(k):
        other = wrap(me + k, tiles)
        pltpu.make_async_remote_copy(
            src_ref=ask.at[other],
            dst_ref=asked.at[me],
            send_sem=ask_send,
            recv_sem=ask_recv,
            device_id=(other, core),
            device_id_type=MESH,
        ).start()

    for_all(tiles, start_ask)
    asked[pl.ds(me, 1)] = ask[pl.ds(me, 1)]

    loads[3].wait()
    for b in range(fblocks):
        tall[b * SUB : b * SUB + channels, :] = inc_ref[:, b * LANES : (b + 1) * LANES].astype(f32)
    fine[...] = jnp.zeros_like(fine)
    planes = [tall[pl.ds(c, fblocks, stride=SUB), :] for c in range(channels)]
    for k in range(part):
        value = planes[k]
        for c in range(1, channels):
            value = jnp.where(first + k == c, planes[c], value)
        fine[:fblocks, k * LANES : (k + 1) * LANES] = value.astype(bf16)

    wide = lax.broadcasted_iota(jnp.int32, (rows, tiles * slots), 1).astype(f32)
    pick[...] = jnp.zeros_like(pick)
    for p in range(pairs):
        slot = jnp.sum(jnp.where(named[p], earlier, 0.0), axis=1, keepdims=True)
        place = owner[:, p : p + 1] * float(slots) + slot
        pick[p * row_pad : p * row_pad + rows, :] = jnp.where(wide == place, 1.0, 0.0).astype(bf16)

    live = [lane < count[:, p : p + 1] for p in range(pairs)]
    spread[...] = jnp.zeros_like(spread)
    ratio[...] = jnp.zeros_like(ratio)
    for p in range(pairs):
        spread[p, pl.ds(ONES, rows, stride=SUB), :] = jnp.where(live[p], 1.0, 0.0)

    chunk = next(n for n in (512, 384, 256, 128) if cells % n == 0)
    sub = lax.broadcasted_iota(jnp.int32, (SUB, chunk), 0)

    def member_stats(ref, base):
        def body(j, carry):
            at = pl.ds(pl.multiple_of(j * chunk, chunk), chunk)
            sums = jnp.zeros((SUB, chunk), f32)
            squares = jnp.zeros((SUB, chunk), f32)
            for c in range(channels):
                values = ref[c, :, at].astype(f32)
                total = jnp.sum(values, axis=0, keepdims=True)
                dev = values - total * (1.0 / members)
                sq = jnp.sum(dev * dev, axis=0, keepdims=True)
                sums = jnp.where(sub == c, total, sums)
                squares = jnp.where(sub == c, sq, squares)
            stats[core, base : base + SUB, at] = sums
            stats[core, base + SUB : base + 2 * SUB, at] = squares
            return carry

        lax.fori_loop(0, cells // chunk, body, 0)

    def wait_all(buffer, sem):
        pltpu.make_async_copy(buffer, buffer, sem).wait()

    loads[4].wait()
    member_stats(prior, 0)

    wait_all(asked.at[: tiles - 1], ask_recv)
    square[...] = jnp.zeros_like(square)
    for t in range(tiles):
        square[t : t + 1, :] = asked[t]
    turned = jnp.transpose(square[...])
    fine_lane = lax.broadcasted_iota(jnp.int32, (slots, fine_pad), 1).astype(f32)
    for t in range(tiles):
        hits[t * slots : (t + 1) * slots, :] = jnp.where(
            turned[:slots, t : t + 1] == fine_lane, 1.0, 0.0
        ).astype(bf16)
    served[...] = jnp.dot(hits[...], fine[...], preferred_element_type=f32).astype(bf16)

    def rows_of(t):
        return pl.ds(pl.multiple_of(t * slots, slots), slots)

    def start_data(k):
        other = wrap(me + wrap(k - 1 + tiles // 2, tiles - 1) + 1, tiles)
        pltpu.make_async_remote_copy(
            src_ref=served.at[rows_of(other)],
            dst_ref=got.at[rows_of(me)],
            send_sem=data_send,
            recv_sem=data_recv,
            device_id=(other, core),
            device_id_type=MESH,
        ).start()

    for_all(tiles, start_data)
    got[rows_of(me), :] = served[rows_of(me), :]

    loads[6].wait()
    member_stats(post, 2 * SUB)

    def core_copy(buffer, send, recv, k, here):
        other = wrap(core + k, mems)
        source = here if here is not None else other
        return pltpu.make_async_remote_copy(
            src_ref=buffer.at[core],
            dst_ref=buffer.at[source],
            send_sem=send.at[other],
            recv_sem=recv.at[source],
            device_id=(me, other),
            device_id_type=MESH,
        )

    for k in range(1, mems):
        core_copy(stats, stat_send, stat_recv, k, core).start()

    loads[5].wait()
    loads[7].wait()

    def remap(r):
        left = jnp.concatenate(
            [spread[p, r * SUB : (r + 1) * SUB, :] for p in range(pairs)], axis=1
        ).astype(bf16)
        right = jnp.concatenate([weight[r, p] for p in range(pairs)], axis=1)
        return lax.dot_general(
            left, right, (((1,), (1,)), ((), ())), preferred_element_type=f32
        )

    for r in range(rows):
        before[r : r + 1, :] = remap(r)[ONES : ONES + 1, :]
    rest = area_ref[...] / before[...]
    for i in range(3):
        rounded = rest.astype(bf16).astype(f32)
        ratio[pl.ds(i, rows, stride=SUB), :] = rounded
        rest = rest - rounded
    for r in range(rows):
        right = jnp.concatenate([weight[r, p] for p in range(pairs)], axis=1)
        share = jnp.dot(
            ratio[r * SUB : (r + 1) * SUB, :].astype(bf16), right, preferred_element_type=f32
        )
        share = jnp.sum(share, axis=0, keepdims=True)
        for p in range(pairs):
            shares[p, r : r + 1, :] = share[:, p * LANES : (p + 1) * LANES]

    for k in range(1, mems):
        core_copy(stats, stat_send, stat_recv, k, None).wait()
    everyone = members * mems
    for j in range(cells // chunk):
        at = slice(j * chunk, (j + 1) * chunk)

        def combined(base):
            sums = [stats[m, base : base + SUB, at] for m in range(mems)]
            mean = functools.reduce(jnp.add, sums) * (1.0 / everyone)
            total = functools.reduce(
                jnp.add, [stats[m, base + SUB : base + 2 * SUB, at] for m in range(mems)]
            )
            for s in sums:
                off = s * (1.0 / members) - mean
                total = total + members * (off * off)
            return mean, jnp.sqrt(total * (1.0 / (everyone - 1)) + variance_eps)

        prior_mean, prior_spread = combined(0)
        post_mean, post_spread = combined(2 * SUB)
        out_ref[0, :, at] = prior_mean
        out_ref[1, :, at] = 1.0 + relax_weight * (prior_spread - post_spread) / post_spread
        out_ref[2, :, at] = post_mean

    wait_all(got.at[: (tiles - 1) * slots], data_recv)
    picked = jnp.dot(pick[...], got[...], preferred_element_type=f32)
    level_lane = lax.broadcasted_iota(jnp.int32, (1, LANES), 1)
    row = jnp.where(level_lane == ONES, jnp.sum(area_ref[...], keepdims=True), 0.0)
    for k in range(part):
        added = jnp.zeros((rows, LANES), f32)
        for p in range(pairs):
            mine = picked[p * row_pad : p * row_pad + rows, k * LANES : (k + 1) * LANES]
            added = added + jnp.where(live[p], mine * shares[p], 0.0)
        here = (level_lane == first + k) & (core * part < channels)
        row = jnp.where(here, jnp.sum(added, keepdims=True), row)
    level[pl.ds(flat, 1)] = row[None]

    def start_level(tile, mem):
        pltpu.make_async_remote_copy(
            src_ref=level.at[flat],
            dst_ref=level.at[flat],
            send_sem=level_send,
            recv_sem=level_recv,
            device_id=(tile, mem),
            device_id_type=MESH,
        ).start()

    for_devices(start_level)

    for p in range(pairs):
        for c in range(channels):
            value = jnp.zeros((rows, LANES), f32)
            for k in range(part):
                mine = picked[p * row_pad : p * row_pad + rows, k * LANES : (k + 1) * LANES]
                value = jnp.where((first + k == c) & (core * part < channels), mine, value)
            spread[p, pl.ds(c, rows, stride=SUB), :] = jnp.where(live[p], value, 0.0)

    pieces = 2
    piece = rows // pieces

    def coarse_copy(i, k, here):
        other = wrap(core + k, mems)
        source = here if here is not None else other
        at = pl.ds(i * piece * LANES, piece * LANES)
        return pltpu.make_async_remote_copy(
            src_ref=coarse.at[core, :, at],
            dst_ref=coarse.at[source, :, at],
            send_sem=coarse_send.at[i, other],
            recv_sem=coarse_recv.at[i, source],
            device_id=(me, other),
            device_id_type=MESH,
        )

    for i in range(pieces):
        for r in range(i * piece, (i + 1) * piece):
            product = remap(r)
            coarse[core, :, r * LANES : (r + 1) * LANES] = product / product[ONES : ONES + 1, :]
        for k in range(1, mems):
            coarse_copy(i, k, core).start()

    for i in range(pieces):
        for k in range(1, mems):
            coarse_copy(i, k, None).wait()
    wait_all(level.at[: devices - 1], level_recv)
    row = level[0]
    for d in range(1, devices):
        row = row + level[d]
    eye = lax.broadcasted_iota(jnp.int32, (SUB, LANES), 0) == lax.broadcasted_iota(
        jnp.int32, (SUB, LANES), 1
    )
    weighted = jnp.sum(jnp.where(eye, row, 0.0), axis=1, keepdims=True)
    area = weighted[ONES : ONES + 1, :] * (1.0 / mems)
    mean = weighted / area
    for j in range(cells // chunk):
        at = slice(j * chunk, (j + 1) * chunk)
        value = functools.reduce(jnp.add, [coarse[m, :, at] for m in range(mems)])
        out_ref[0, :, at] = out_ref[0, :, at] + (value - mean)
    wait_all(asked.at[: tiles - 1], ask_send)
    wait_all(got.at[: (tiles - 1) * slots], data_send)
    wait_all(level.at[: devices - 1], level_send)


def per_device(
    inc_fine, pair_owner, pair_block, pair_count, pair_weight, cell_area, prior, posterior
):
    tiles = lax.axis_size("tile")
    mems = lax.axis_size("mem")
    channels, fine_cells = inc_fine.shape
    rows, pairs = pair_owner.shape
    cells = prior.shape[2]
    fblocks = fine_cells // LANES
    cap = max(2, (2 * rows * pairs + tiles - 1) // tiles)
    cap = min(cap, rows)
    slots = round_up(cap, 16)
    part = -(-channels // mems)
    fine_pad = round_up(fblocks, LANES)
    row_pad = round_up(rows, 16)
    devices = tiles * mems
    vmem = pl.BlockSpec(memory_space=pltpu.VMEM)
    hbm = pl.BlockSpec(memory_space=pltpu.HBM)
    dma = pltpu.SemaphoreType.DMA
    small = pl.pallas_call(
        functools.partial(kernel, tiles, mems, cap),
        out_shape=pltpu.VMEM((3, SUB, cells), f32),
        in_specs=[hbm] * 8,
        out_specs=vmem,
        scratch_shapes=[
            pltpu.VMEM(inc_fine.shape, bf16),
            pltpu.VMEM((3, pairs, rows), jnp.int32),
            pltpu.VMEM((rows, LANES), f32),
            pltpu.VMEM(pair_weight.shape, bf16),
            pltpu.VMEM(prior.shape, bf16),
            pltpu.VMEM(posterior.shape, bf16),
            pltpu.VMEM((fblocks * SUB, LANES), f32),
            pltpu.VMEM((fine_pad, part * LANES), bf16),
            pltpu.VMEM((rows, LANES), f32),
            pltpu.VMEM((LANES, LANES), f32),
            pltpu.VMEM((tiles * slots, fine_pad), bf16),
            pltpu.VMEM((tiles, 1, LANES), f32),
            pltpu.VMEM((tiles, 1, LANES), f32),
            pltpu.VMEM((pairs * row_pad, tiles * slots), bf16),
            pltpu.VMEM((tiles * slots, part * LANES), bf16),
            pltpu.VMEM((tiles * slots, part * LANES), bf16),
            pltpu.VMEM((pairs, rows * SUB, LANES), f32),
            pltpu.VMEM((rows * SUB, LANES), f32),
            pltpu.VMEM((pairs, rows, LANES), f32),
            pltpu.VMEM((mems, 4 * SUB, cells), f32),
            pltpu.VMEM((mems, SUB, cells), f32),
            pltpu.VMEM((devices, 1, LANES), f32),
            dma((8,)),
            dma,
            dma,
            dma,
            dma,
            dma((mems,)),
            dma((mems,)),
            dma((2, mems)),
            dma((2, mems)),
            dma,
            dma,
        ],
        compiler_params=pltpu.CompilerParams(
            collective_id=0, has_side_effects=True, vmem_limit_bytes=56 * 1024 * 1024
        ),
        name="remap_and_spread",
    )(
        inc_fine,
        pair_owner.T,
        pair_block.T,
        pair_count.T,
        cell_area.reshape(rows, -1),
        pair_weight,
        prior,
        posterior,
    )
    center, factor, post_mean = (small[i, :channels, None, :] for i in range(3))
    return (center + factor * (posterior.astype(f32) - post_mean)).astype(bf16)


def solution(mesh):
    in_specs = (
        P(None, "tile"),
        P("tile", None),
        P("tile", None),
        P("tile", None),
        P("tile", None, None, None),
        P("tile"),
        P(None, "mem", "tile"),
        P(None, "mem", "tile"),
    )
    out_specs = P(None, "mem", "tile")
    return jax.shard_map(
        per_device, mesh=mesh, in_specs=in_specs, out_specs=out_specs, check_vma=False
    )
```

```python
import functools

import jax
import jax.numpy as jnp
from jax import lax
from jax.experimental import pallas as pl
from jax.experimental.pallas import tpu as pltpu
from jax.sharding import PartitionSpec as P

relax_weight = 0.85
variance_eps = 1e-06
f32 = jnp.float32
bf16 = jnp.bfloat16
MESH = pl.DeviceIdType.MESH
LANES = 128
SUB = 8
ONES = 7


def round_up(n, k):
    return -(-n // k) * k


def kernel(
    tiles,
    mems,
    cap,
    inc_hbm,
    owner_hbm,
    block_hbm,
    count_hbm,
    area_hbm,
    weight_hbm,
    prior_hbm,
    post_hbm,
    out_ref,
    inc_ref,
    index,
    area_ref,
    weight,
    prior,
    post,
    tall,
    fine,
    before,
    square,
    hits,
    ask,
    asked,
    pick,
    served,
    got,
    spread,
    ratio,
    shares,
    stats,
    coarse,
    level,
    whole,
    local_sem,
    ask_send,
    ask_recv,
    data_send,
    data_recv,
    stat_send,
    stat_recv,
    coarse_send,
    coarse_recv,
    level_send,
    level_recv,
    whole_send,
    whole_recv,
):
    channels = inc_ref.shape[0]
    pairs, rows = owner_hbm.shape
    fblocks = inc_ref.shape[1] // LANES
    fine_pad = fine.shape[0]
    part = got.shape[1] // LANES
    slots = got.shape[0] // tiles
    row_pad = pick.shape[0] // pairs
    members, cells = prior.shape[1], prior.shape[2]
    me = lax.axis_index("tile")
    core = lax.axis_index("mem")
    first = jnp.minimum(core * part, channels - part)

    def wrap(n, size):
        return jnp.where(n >= size, n - size, n)

    def for_all(size, action):
        def body(k, carry):
            action(k)
            return carry

        lax.fori_loop(1, size, body, 0)

    loads = [
        pltpu.make_async_copy(source, target, local_sem.at[i])
        for i, (source, target) in enumerate(
            [
                (owner_hbm, index.at[0]),
                (block_hbm, index.at[1]),
                (count_hbm, index.at[2]),
                (inc_hbm, inc_ref),
                (prior_hbm, prior),
                (weight_hbm, weight),
                (post_hbm, post),
                (area_hbm, area_ref),
            ]
        )
    ]
    for load in loads[:4]:
        load.start()

    barrier = pltpu.get_barrier_semaphore()

    def greet(tile, mem):
        pl.semaphore_signal(barrier, inc=1, device_id=(tile, mem), device_id_type=MESH)

    for_all(tiles, lambda k: greet(wrap(me + k, tiles), core))
    for k in range(1, mems):
        greet(me, wrap(core + k, mems))
    for load in loads[4:]:
        load.start()

    lane = lax.broadcasted_iota(jnp.int32, (rows, LANES), 1).astype(f32)
    square[...] = jnp.zeros_like(square)
    for load in loads[:3]:
        load.wait()
    for i in range(3):
        square[i * SUB : i * SUB + pairs, :rows] = index[i].astype(f32)
    turned = jnp.transpose(square[...])[:rows]
    owner, block, count = (turned[:, i * SUB : i * SUB + pairs] for i in range(3))
    named = [owner[:, p : p + 1] == lane for p in range(pairs)]
    any_named = jnp.zeros((rows, LANES), f32)
    wanted = jnp.zeros((rows, LANES), f32)
    for p in range(pairs):
        any_named = any_named + jnp.where(named[p], 1.0, 0.0)
        wanted = wanted + jnp.where(named[p], block[:, p : p + 1] + 1.0, 0.0)
    run = jnp.zeros((1, LANES), f32)
    for r in range(rows):
        before[r : r + 1, :] = run
        run = run + any_named[r : r + 1, :]
    earlier = before[...]
    square[...] = jnp.zeros_like(square)
    for s in range(cap):
        chosen = jnp.where((earlier == float(s)) & (any_named > 0.0), wanted, 0.0)
        square[s : s + 1, :] = jnp.sum(chosen, axis=0, keepdims=True)
    turned = jnp.transpose(square[...]) - 1.0
    for t in range(tiles):
        ask[t] = turned[t : t + 1, :]

    pl.semaphore_wait(barrier, tiles + mems - 2)

    def start_ask(k):
        other = wrap(me + k, tiles)
        pltpu.make_async_remote_copy(
            src_ref=ask.at[other],
            dst_ref=asked.at[me],
            send_sem=ask_send,
            recv_sem=ask_recv,
            device_id=(other, core),
            device_id_type=MESH,
        ).start()

    for_all(tiles, start_ask)
    asked[pl.ds(me, 1)] = ask[pl.ds(me, 1)]

    loads[3].wait()
    for b in range(fblocks):
        tall[b * SUB : b * SUB + channels, :] = inc_ref[:, b * LANES : (b + 1) * LANES].astype(f32)
    fine[...] = jnp.zeros_like(fine)
    planes = [tall[pl.ds(c, fblocks, stride=SUB), :] for c in range(channels)]
    for k in range(part):
        value = planes[k]
        for c in range(1, channels):
            value = jnp.where(first + k == c, planes[c], value)
        fine[:fblocks, k * LANES : (k + 1) * LANES] = value.astype(bf16)

    wide = lax.broadcasted_iota(jnp.int32, (rows, tiles * slots), 1).astype(f32)
    pick[...] = jnp.zeros_like(pick)
    for p in range(pairs):
        slot = jnp.sum(jnp.where(named[p], earlier, 0.0), axis=1, keepdims=True)
        place = owner[:, p : p + 1] * float(slots) + slot
        pick[p * row_pad : p * row_pad + rows, :] = jnp.where(wide == place, 1.0, 0.0).astype(bf16)

    live = [lane < count[:, p : p + 1] for p in range(pairs)]
    spread[...] = jnp.zeros_like(spread)
    ratio[...] = jnp.zeros_like(ratio)
    for p in range(pairs):
        spread[p, pl.ds(ONES, rows, stride=SUB), :] = jnp.where(live[p], 1.0, 0.0)

    chunk = next(n for n in (512, 384, 256, 128) if cells % n == 0)
    sub = lax.broadcasted_iota(jnp.int32, (SUB, chunk), 0)

    def member_stats(ref, base):
        def body(j, carry):
            at = pl.ds(pl.multiple_of(j * chunk, chunk), chunk)
            sums = jnp.zeros((SUB, chunk), f32)
            squares = jnp.zeros((SUB, chunk), f32)
            for c in range(channels):
                values = ref[c, :, at].astype(f32)
                total = jnp.sum(values, axis=0, keepdims=True)
                dev = values - total * (1.0 / members)
                sq = jnp.sum(dev * dev, axis=0, keepdims=True)
                sums = jnp.where(sub == c, total, sums)
                squares = jnp.where(sub == c, sq, squares)
            stats[core, base : base + SUB, at] = sums
            stats[core, base + SUB : base + 2 * SUB, at] = squares
            return carry

        lax.fori_loop(0, cells // chunk, body, 0)

    def wait_all(buffer, sem):
        pltpu.make_async_copy(buffer, buffer, sem).wait()

    loads[4].wait()
    member_stats(prior, 0)

    wait_all(asked.at[: tiles - 1], ask_recv)
    square[...] = jnp.zeros_like(square)
    for t in range(tiles):
        square[t : t + 1, :] = asked[t]
    turned = jnp.transpose(square[...])
    fine_lane = lax.broadcasted_iota(jnp.int32, (slots, fine_pad), 1).astype(f32)
    for t in range(tiles):
        hits[t * slots : (t + 1) * slots, :] = jnp.where(
            turned[:slots, t : t + 1] == fine_lane, 1.0, 0.0
        ).astype(bf16)
    served[...] = jnp.dot(hits[...], fine[...], preferred_element_type=f32).astype(bf16)

    def rows_of(t):
        return pl.ds(pl.multiple_of(t * slots, slots), slots)

    def start_data(k):
        other = wrap(me + wrap(k - 1 + tiles // 2, tiles - 1) + 1, tiles)
        pltpu.make_async_remote_copy(
            src_ref=served.at[rows_of(other)],
            dst_ref=got.at[rows_of(me)],
            send_sem=data_send,
            recv_sem=data_recv,
            device_id=(other, core),
            device_id_type=MESH,
        ).start()

    for_all(tiles, start_data)
    got[rows_of(me), :] = served[rows_of(me), :]

    loads[6].wait()
    member_stats(post, 2 * SUB)

    def core_copy(buffer, send, recv, k, here):
        other = wrap(core + k, mems)
        source = here if here is not None else other
        return pltpu.make_async_remote_copy(
            src_ref=buffer.at[core],
            dst_ref=buffer.at[source],
            send_sem=send.at[other],
            recv_sem=recv.at[source],
            device_id=(me, other),
            device_id_type=MESH,
        )

    for k in range(1, mems):
        core_copy(stats, stat_send, stat_recv, k, core).start()

    loads[5].wait()
    loads[7].wait()

    def remap(r):
        left = jnp.concatenate(
            [spread[p, r * SUB : (r + 1) * SUB, :] for p in range(pairs)], axis=1
        ).astype(bf16)
        right = jnp.concatenate([weight[r, p] for p in range(pairs)], axis=1)
        return lax.dot_general(
            left, right, (((1,), (1,)), ((), ())), preferred_element_type=f32
        )

    for r in range(rows):
        before[r : r + 1, :] = remap(r)[ONES : ONES + 1, :]
    rest = area_ref[...] / before[...]
    for i in range(3):
        rounded = rest.astype(bf16).astype(f32)
        ratio[pl.ds(i, rows, stride=SUB), :] = rounded
        rest = rest - rounded
    for r in range(rows):
        right = jnp.concatenate([weight[r, p] for p in range(pairs)], axis=1)
        share = jnp.dot(
            ratio[r * SUB : (r + 1) * SUB, :].astype(bf16), right, preferred_element_type=f32
        )
        share = jnp.sum(share, axis=0, keepdims=True)
        for p in range(pairs):
            shares[p, r : r + 1, :] = share[:, p * LANES : (p + 1) * LANES]

    for k in range(1, mems):
        core_copy(stats, stat_send, stat_recv, k, None).wait()
    everyone = members * mems
    for j in range(cells // chunk):
        at = slice(j * chunk, (j + 1) * chunk)

        def combined(base):
            sums = [stats[m, base : base + SUB, at] for m in range(mems)]
            mean = functools.reduce(jnp.add, sums) * (1.0 / everyone)
            total = functools.reduce(
                jnp.add, [stats[m, base + SUB : base + 2 * SUB, at] for m in range(mems)]
            )
            for s in sums:
                off = s * (1.0 / members) - mean
                total = total + members * (off * off)
            return mean, jnp.sqrt(total * (1.0 / (everyone - 1)) + variance_eps)

        prior_mean, prior_spread = combined(0)
        post_mean, post_spread = combined(2 * SUB)
        out_ref[0, :, at] = prior_mean
        out_ref[1, :, at] = 1.0 + relax_weight * (prior_spread - post_spread) / post_spread
        out_ref[2, :, at] = post_mean

    wait_all(got.at[: (tiles - 1) * slots], data_recv)
    picked = jnp.dot(pick[...], got[...], preferred_element_type=f32)
    level_lane = lax.broadcasted_iota(jnp.int32, (1, LANES), 1)
    row = jnp.where(level_lane == ONES, jnp.sum(area_ref[...], keepdims=True), 0.0)
    for k in range(part):
        added = jnp.zeros((rows, LANES), f32)
        for p in range(pairs):
            mine = picked[p * row_pad : p * row_pad + rows, k * LANES : (k + 1) * LANES]
            added = added + jnp.where(live[p], mine * shares[p], 0.0)
        here = (level_lane == first + k) & (core * part < channels)
        row = jnp.where(here, jnp.sum(added, keepdims=True), row)
    level[pl.ds(me, 1)] = row[None]

    def start_level(k):
        pltpu.make_async_remote_copy(
            src_ref=level.at[me],
            dst_ref=level.at[me],
            send_sem=level_send,
            recv_sem=level_recv,
            device_id=(wrap(me + k, tiles), core),
            device_id_type=MESH,
        ).start()

    for_all(tiles, start_level)

    for p in range(pairs):
        for c in range(channels):
            value = jnp.zeros((rows, LANES), f32)
            for k in range(part):
                mine = picked[p * row_pad : p * row_pad + rows, k * LANES : (k + 1) * LANES]
                value = jnp.where((first + k == c) & (core * part < channels), mine, value)
            spread[p, pl.ds(c, rows, stride=SUB), :] = jnp.where(live[p], value, 0.0)

    pieces = 2
    piece = rows // pieces

    def coarse_copy(i, k, here):
        other = wrap(core + k, mems)
        source = here if here is not None else other
        at = pl.ds(i * piece * LANES, piece * LANES)
        return pltpu.make_async_remote_copy(
            src_ref=coarse.at[core, :, at],
            dst_ref=coarse.at[source, :, at],
            send_sem=coarse_send.at[i, other],
            recv_sem=coarse_recv.at[i, source],
            device_id=(me, other),
            device_id_type=MESH,
        )

    for i in range(pieces):
        for r in range(i * piece, (i + 1) * piece):
            product = remap(r)
            coarse[core, :, r * LANES : (r + 1) * LANES] = product / product[ONES : ONES + 1, :]
        for k in range(1, mems):
            coarse_copy(i, k, core).start()

    wait_all(level.at[: tiles - 1], level_recv)
    row = level[0]
    for t in range(1, tiles):
        row = row + level[t]
    whole[pl.ds(core, 1)] = row[None]
    for k in range(1, mems):
        core_copy(whole, whole_send, whole_recv, k, core).start()
    for i in range(pieces):
        for k in range(1, mems):
            coarse_copy(i, k, None).wait()
    for k in range(1, mems):
        core_copy(whole, whole_send, whole_recv, k, None).wait()
    row = whole[0]
    for m in range(1, mems):
        row = row + whole[m]
    eye = lax.broadcasted_iota(jnp.int32, (SUB, LANES), 0) == lax.broadcasted_iota(
        jnp.int32, (SUB, LANES), 1
    )
    weighted = jnp.sum(jnp.where(eye, row, 0.0), axis=1, keepdims=True)
    area = weighted[ONES : ONES + 1, :] * (1.0 / mems)
    mean = weighted / area
    for j in range(cells // chunk):
        at = slice(j * chunk, (j + 1) * chunk)
        value = functools.reduce(jnp.add, [coarse[m, :, at] for m in range(mems)])
        out_ref[0, :, at] = out_ref[0, :, at] + (value - mean)
    wait_all(asked.at[: tiles - 1], ask_send)
    wait_all(got.at[: (tiles - 1) * slots], data_send)
    wait_all(level.at[: tiles - 1], level_send)


def per_device(
    inc_fine, pair_owner, pair_block, pair_count, pair_weight, cell_area, prior, posterior
):
    tiles = lax.axis_size("tile")
    mems = lax.axis_size("mem")
    channels, fine_cells = inc_fine.shape
    rows, pairs = pair_owner.shape
    cells = prior.shape[2]
    fblocks = fine_cells // LANES
    cap = max(2, (2 * rows * pairs + tiles - 1) // tiles)
    cap = min(cap, rows)
    slots = round_up(cap, 16)
    part = -(-channels // mems)
    fine_pad = round_up(fblocks, LANES)
    row_pad = round_up(rows, 16)
    vmem = pl.BlockSpec(memory_space=pltpu.VMEM)
    hbm = pl.BlockSpec(memory_space=pltpu.HBM)
    dma = pltpu.SemaphoreType.DMA
    small = pl.pallas_call(
        functools.partial(kernel, tiles, mems, cap),
        out_shape=pltpu.VMEM((3, SUB, cells), f32),
        in_specs=[hbm] * 8,
        out_specs=vmem,
        scratch_shapes=[
            pltpu.VMEM(inc_fine.shape, bf16),
            pltpu.VMEM((3, pairs, rows), jnp.int32),
            pltpu.VMEM((rows, LANES), f32),
            pltpu.VMEM(pair_weight.shape, bf16),
            pltpu.VMEM(prior.shape, bf16),
            pltpu.VMEM(posterior.shape, bf16),
            pltpu.VMEM((fblocks * SUB, LANES), f32),
            pltpu.VMEM((fine_pad, part * LANES), bf16),
            pltpu.VMEM((rows, LANES), f32),
            pltpu.VMEM((LANES, LANES), f32),
            pltpu.VMEM((tiles * slots, fine_pad), bf16),
            pltpu.VMEM((tiles, 1, LANES), f32),
            pltpu.VMEM((tiles, 1, LANES), f32),
            pltpu.VMEM((pairs * row_pad, tiles * slots), bf16),
            pltpu.VMEM((tiles * slots, part * LANES), bf16),
            pltpu.VMEM((tiles * slots, part * LANES), bf16),
            pltpu.VMEM((pairs, rows * SUB, LANES), f32),
            pltpu.VMEM((rows * SUB, LANES), f32),
            pltpu.VMEM((pairs, rows, LANES), f32),
            pltpu.VMEM((mems, 4 * SUB, cells), f32),
            pltpu.VMEM((mems, SUB, cells), f32),
            pltpu.VMEM((tiles, 1, LANES), f32),
            pltpu.VMEM((mems, 1, LANES), f32),
            dma((8,)),
            dma,
            dma,
            dma,
            dma,
            dma((mems,)),
            dma((mems,)),
            dma((2, mems)),
            dma((2, mems)),
            dma,
            dma,
            dma((mems,)),
            dma((mems,)),
        ],
        compiler_params=pltpu.CompilerParams(
            collective_id=0, has_side_effects=True, vmem_limit_bytes=56 * 1024 * 1024
        ),
        name="remap_and_spread",
    )(
        inc_fine,
        pair_owner.T,
        pair_block.T,
        pair_count.T,
        cell_area.reshape(rows, -1),
        pair_weight,
        prior,
        posterior,
    )
    center, factor, post_mean = (small[i, :channels, None, :] for i in range(3))
    return (center + factor * (posterior.astype(f32) - post_mean)).astype(bf16)


def solution(mesh):
    in_specs = (
        P(None, "tile"),
        P("tile", None),
        P("tile", None),
        P("tile", None),
        P("tile", None, None, None),
        P("tile"),
        P(None, "mem", "tile"),
        P(None, "mem", "tile"),
    )
    out_specs = P(None, "mem", "tile")
    return jax.shard_map(
        per_device, mesh=mesh, in_specs=in_specs, out_specs=out_specs, check_vma=False
    )
```

```python
import functools

import jax
import jax.numpy as jnp
from jax import lax
from jax.experimental import pallas as pl
from jax.experimental.pallas import tpu as pltpu
from jax.sharding import PartitionSpec as P

relax_weight = 0.85
variance_eps = 1e-06
f32 = jnp.float32
bf16 = jnp.bfloat16
MESH = pl.DeviceIdType.MESH
LANES = 128
SUB = 8
ONES = 7


def round_up(n, k):
    return -(-n // k) * k


def kernel(
    tiles,
    mems,
    cap,
    inc_hbm,
    owner_hbm,
    block_hbm,
    count_hbm,
    area_hbm,
    weight_hbm,
    prior_hbm,
    post_hbm,
    out_ref,
    inc_ref,
    index,
    area_ref,
    weight,
    prior,
    post,
    tall,
    fine,
    before,
    square,
    hits,
    ask,
    asked,
    pick,
    served,
    got,
    spread,
    ratio,
    shares,
    stats,
    coarse,
    level,
    whole,
    local_sem,
    ask_send,
    ask_recv,
    data_send,
    data_recv,
    stat_send,
    stat_recv,
    coarse_send,
    coarse_recv,
    level_send,
    level_recv,
    whole_send,
    whole_recv,
    share_send,
    share_recv,
):
    channels = inc_ref.shape[0]
    pairs, rows = owner_hbm.shape
    fblocks = inc_ref.shape[1] // LANES
    fine_pad = fine.shape[0]
    part = got.shape[1] // LANES
    slots = got.shape[0] // tiles
    row_pad = pick.shape[0] // pairs
    members, cells = prior.shape[1], prior.shape[2]
    me = lax.axis_index("tile")
    core = lax.axis_index("mem")
    first = jnp.minimum(core * part, channels - part)

    def wrap(n, size):
        return jnp.where(n >= size, n - size, n)

    def for_all(size, action):
        def body(k, carry):
            action(k)
            return carry

        lax.fori_loop(1, size, body, 0)

    loads = [
        pltpu.make_async_copy(source, target, local_sem.at[i])
        for i, (source, target) in enumerate(
            [
                (owner_hbm, index.at[0]),
                (block_hbm, index.at[1]),
                (count_hbm, index.at[2]),
                (inc_hbm, inc_ref),
                (prior_hbm, prior),
                (weight_hbm, weight),
                (post_hbm, post),
                (area_hbm, area_ref),
            ]
        )
    ]
    for load in loads[:4]:
        load.start()

    barrier = pltpu.get_barrier_semaphore()

    def greet(tile, mem):
        pl.semaphore_signal(barrier, inc=1, device_id=(tile, mem), device_id_type=MESH)

    for_all(tiles, lambda k: greet(wrap(me + k, tiles), core))
    for k in range(1, mems):
        greet(me, wrap(core + k, mems))
    for load in loads[4:]:
        load.start()

    lane = lax.broadcasted_iota(jnp.int32, (rows, LANES), 1).astype(f32)
    square[...] = jnp.zeros_like(square)
    for load in loads[:3]:
        load.wait()
    for i in range(3):
        square[i * SUB : i * SUB + pairs, :rows] = index[i].astype(f32)
    turned = jnp.transpose(square[...])[:rows]
    owner, block, count = (turned[:, i * SUB : i * SUB + pairs] for i in range(3))
    named = [owner[:, p : p + 1] == lane for p in range(pairs)]
    any_named = jnp.zeros((rows, LANES), f32)
    wanted = jnp.zeros((rows, LANES), f32)
    for p in range(pairs):
        any_named = any_named + jnp.where(named[p], 1.0, 0.0)
        wanted = wanted + jnp.where(named[p], block[:, p : p + 1] + 1.0, 0.0)
    run = jnp.zeros((1, LANES), f32)
    for r in range(rows):
        before[r : r + 1, :] = run
        run = run + any_named[r : r + 1, :]
    earlier = before[...]
    square[...] = jnp.zeros_like(square)
    for s in range(cap):
        chosen = jnp.where((earlier == float(s)) & (any_named > 0.0), wanted, 0.0)
        square[s : s + 1, :] = jnp.sum(chosen, axis=0, keepdims=True)
    turned = jnp.transpose(square[...]) - 1.0
    for t in range(tiles):
        ask[t] = turned[t : t + 1, :]

    pl.semaphore_wait(barrier, tiles + mems - 2)

    def start_ask(k):
        other = wrap(me + k, tiles)
        pltpu.make_async_remote_copy(
            src_ref=ask.at[other],
            dst_ref=asked.at[me],
            send_sem=ask_send,
            recv_sem=ask_recv,
            device_id=(other, core),
            device_id_type=MESH,
        ).start()

    for_all(tiles, start_ask)
    asked[pl.ds(me, 1)] = ask[pl.ds(me, 1)]

    loads[3].wait()
    for b in range(fblocks):
        tall[b * SUB : b * SUB + channels, :] = inc_ref[:, b * LANES : (b + 1) * LANES].astype(f32)
    fine[...] = jnp.zeros_like(fine)
    planes = [tall[pl.ds(c, fblocks, stride=SUB), :] for c in range(channels)]
    for k in range(part):
        value = planes[k]
        for c in range(1, channels):
            value = jnp.where(first + k == c, planes[c], value)
        fine[:fblocks, k * LANES : (k + 1) * LANES] = value.astype(bf16)

    wide = lax.broadcasted_iota(jnp.int32, (rows, tiles * slots), 1).astype(f32)
    pick[...] = jnp.zeros_like(pick)
    for p in range(pairs):
        slot = jnp.sum(jnp.where(named[p], earlier, 0.0), axis=1, keepdims=True)
        place = owner[:, p : p + 1] * float(slots) + slot
        pick[p * row_pad : p * row_pad + rows, :] = jnp.where(wide == place, 1.0, 0.0).astype(bf16)

    live = [lane < count[:, p : p + 1] for p in range(pairs)]
    spread[...] = jnp.zeros_like(spread)
    ratio[...] = jnp.zeros_like(ratio)
    for p in range(pairs):
        spread[p, pl.ds(ONES, rows, stride=SUB), :] = jnp.where(live[p], 1.0, 0.0)

    chunk = next(n for n in (512, 384, 256, 128) if cells % n == 0)
    sub = lax.broadcasted_iota(jnp.int32, (SUB, chunk), 0)

    def member_stats(ref, base):
        def body(j, carry):
            at = pl.ds(pl.multiple_of(j * chunk, chunk), chunk)
            sums = jnp.zeros((SUB, chunk), f32)
            squares = jnp.zeros((SUB, chunk), f32)
            for c in range(channels):
                values = ref[c, :, at].astype(f32)
                total = jnp.sum(values, axis=0, keepdims=True)
                dev = values - total * (1.0 / members)
                sq = jnp.sum(dev * dev, axis=0, keepdims=True)
                sums = jnp.where(sub == c, total, sums)
                squares = jnp.where(sub == c, sq, squares)
            stats[core, base : base + SUB, at] = sums
            stats[core, base + SUB : base + 2 * SUB, at] = squares
            return carry

        lax.fori_loop(0, cells // chunk, body, 0)

    def wait_all(buffer, sem):
        pltpu.make_async_copy(buffer, buffer, sem).wait()

    loads[4].wait()
    member_stats(prior, 0)

    wait_all(asked.at[: tiles - 1], ask_recv)
    square[...] = jnp.zeros_like(square)
    for t in range(tiles):
        square[t : t + 1, :] = asked[t]
    turned = jnp.transpose(square[...])
    fine_lane = lax.broadcasted_iota(jnp.int32, (slots, fine_pad), 1).astype(f32)
    for t in range(tiles):
        hits[t * slots : (t + 1) * slots, :] = jnp.where(
            turned[:slots, t : t + 1] == fine_lane, 1.0, 0.0
        ).astype(bf16)
    served[...] = jnp.dot(hits[...], fine[...], preferred_element_type=f32).astype(bf16)

    def rows_of(t):
        return pl.ds(pl.multiple_of(t * slots, slots), slots)

    def start_data(k):
        other = wrap(me + wrap(k - 1 + tiles // 2, tiles - 1) + 1, tiles)
        pltpu.make_async_remote_copy(
            src_ref=served.at[rows_of(other)],
            dst_ref=got.at[rows_of(me)],
            send_sem=data_send,
            recv_sem=data_recv,
            device_id=(other, core),
            device_id_type=MESH,
        ).start()

    for_all(tiles, start_data)
    got[rows_of(me), :] = served[rows_of(me), :]

    loads[6].wait()
    member_stats(post, 2 * SUB)

    def core_copy(buffer, send, recv, k, here):
        other = wrap(core + k, mems)
        source = here if here is not None else other
        return pltpu.make_async_remote_copy(
            src_ref=buffer.at[core],
            dst_ref=buffer.at[source],
            send_sem=send.at[other],
            recv_sem=recv.at[source],
            device_id=(me, other),
            device_id_type=MESH,
        )

    for k in range(1, mems):
        core_copy(stats, stat_send, stat_recv, k, core).start()

    loads[5].wait()
    loads[7].wait()

    def rows_at(r):
        return pl.ds(r * SUB if isinstance(r, int) else pl.multiple_of(r * SUB, SUB), SUB)

    def remap(r):
        left = jnp.concatenate(
            [spread[p, rows_at(r), :] for p in range(pairs)], axis=1
        ).astype(bf16)
        right = jnp.concatenate([weight[r, p] for p in range(pairs)], axis=1)
        return lax.dot_general(
            left, right, (((1,), (1,)), ((), ())), preferred_element_type=f32
        )

    own_rows = rows // mems
    before[...] = jnp.ones_like(before)
    shares[core] = jnp.zeros(shares.shape[1:], f32)
    for i in range(own_rows):
        r = core * own_rows + i
        before[pl.ds(r, 1), :] = remap(r)[ONES : ONES + 1, :]
    rest = area_ref[...] / before[...]
    for i in range(3):
        rounded = rest.astype(bf16).astype(f32)
        ratio[pl.ds(i, rows, stride=SUB), :] = rounded
        rest = rest - rounded
    for i in range(own_rows):
        r = core * own_rows + i
        right = jnp.concatenate([weight[r, p] for p in range(pairs)], axis=1)
        left = ratio[pl.ds(pl.multiple_of(r * SUB, SUB), SUB), :].astype(bf16)
        share = jnp.dot(left, right, preferred_element_type=f32)
        share = jnp.sum(share, axis=0, keepdims=True)
        for p in range(pairs):
            shares[core, p, i : i + 1, :] = share[:, p * LANES : (p + 1) * LANES]
    for k in range(1, mems):
        core_copy(shares, share_send, share_recv, k, core).start()

    for k in range(1, mems):
        core_copy(stats, stat_send, stat_recv, k, None).wait()
    everyone = members * mems
    for j in range(cells // chunk):
        at = slice(j * chunk, (j + 1) * chunk)

        def combined(base):
            sums = [stats[m, base : base + SUB, at] for m in range(mems)]
            mean = functools.reduce(jnp.add, sums) * (1.0 / everyone)
            total = functools.reduce(
                jnp.add, [stats[m, base + SUB : base + 2 * SUB, at] for m in range(mems)]
            )
            for s in sums:
                off = s * (1.0 / members) - mean
                total = total + members * (off * off)
            return mean, jnp.sqrt(total * (1.0 / (everyone - 1)) + variance_eps)

        prior_mean, prior_spread = combined(0)
        post_mean, post_spread = combined(2 * SUB)
        out_ref[0, :, at] = prior_mean
        out_ref[1, :, at] = 1.0 + relax_weight * (prior_spread - post_spread) / post_spread
        out_ref[2, :, at] = post_mean

    for k in range(1, mems):
        core_copy(shares, share_send, share_recv, k, None).wait()
    every = [
        jnp.concatenate([shares[m, p, :own_rows, :] for m in range(mems)], axis=0)
        for p in range(pairs)
    ]

    wait_all(got.at[: (tiles - 1) * slots], data_recv)
    picked = jnp.dot(pick[...], got[...], preferred_element_type=f32)
    level_lane = lax.broadcasted_iota(jnp.int32, (1, LANES), 1)
    row = jnp.where(level_lane == ONES, jnp.sum(area_ref[...], keepdims=True), 0.0)
    for k in range(part):
        added = jnp.zeros((rows, LANES), f32)
        for p in range(pairs):
            mine = picked[p * row_pad : p * row_pad + rows, k * LANES : (k + 1) * LANES]
            added = added + jnp.where(live[p], mine * every[p], 0.0)
        here = (level_lane == first + k) & (core * part < channels)
        row = jnp.where(here, jnp.sum(added, keepdims=True), row)
    level[pl.ds(me, 1)] = row[None]

    def start_level(k):
        pltpu.make_async_remote_copy(
            src_ref=level.at[me],
            dst_ref=level.at[me],
            send_sem=level_send,
            recv_sem=level_recv,
            device_id=(wrap(me + k, tiles), core),
            device_id_type=MESH,
        ).start()

    for_all(tiles, start_level)

    for p in range(pairs):
        for c in range(channels):
            value = jnp.zeros((rows, LANES), f32)
            for k in range(part):
                mine = picked[p * row_pad : p * row_pad + rows, k * LANES : (k + 1) * LANES]
                value = jnp.where((first + k == c) & (core * part < channels), mine, value)
            spread[p, pl.ds(c, rows, stride=SUB), :] = jnp.where(live[p], value, 0.0)

    pieces = 2
    piece = rows // pieces

    def coarse_copy(i, k, here):
        other = wrap(core + k, mems)
        source = here if here is not None else other
        at = pl.ds(i * piece * LANES, piece * LANES)
        return pltpu.make_async_remote_copy(
            src_ref=coarse.at[core, :, at],
            dst_ref=coarse.at[source, :, at],
            send_sem=coarse_send.at[i, other],
            recv_sem=coarse_recv.at[i, source],
            device_id=(me, other),
            device_id_type=MESH,
        )

    for i in range(pieces):
        for r in range(i * piece, (i + 1) * piece):
            product = remap(r)
            coarse[core, :, r * LANES : (r + 1) * LANES] = product / product[ONES : ONES + 1, :]
        for k in range(1, mems):
            coarse_copy(i, k, core).start()

    wait_all(level.at[: tiles - 1], level_recv)
    row = level[0]
    for t in range(1, tiles):
        row = row + level[t]
    whole[pl.ds(core, 1)] = row[None]
    for k in range(1, mems):
        core_copy(whole, whole_send, whole_recv, k, core).start()
    for i in range(pieces):
        for k in range(1, mems):
            coarse_copy(i, k, None).wait()
    for k in range(1, mems):
        core_copy(whole, whole_send, whole_recv, k, None).wait()
    row = whole[0]
    for m in range(1, mems):
        row = row + whole[m]
    eye = lax.broadcasted_iota(jnp.int32, (SUB, LANES), 0) == lax.broadcasted_iota(
        jnp.int32, (SUB, LANES), 1
    )
    weighted = jnp.sum(jnp.where(eye, row, 0.0), axis=1, keepdims=True)
    area = weighted[ONES : ONES + 1, :] * (1.0 / mems)
    mean = weighted / area
    for j in range(cells // chunk):
        at = slice(j * chunk, (j + 1) * chunk)
        value = functools.reduce(jnp.add, [coarse[m, :, at] for m in range(mems)])
        out_ref[0, :, at] = out_ref[0, :, at] + (value - mean)
    wait_all(asked.at[: tiles - 1], ask_send)
    wait_all(got.at[: (tiles - 1) * slots], data_send)
    wait_all(level.at[: tiles - 1], level_send)


def per_device(
    inc_fine, pair_owner, pair_block, pair_count, pair_weight, cell_area, prior, posterior
):
    tiles = lax.axis_size("tile")
    mems = lax.axis_size("mem")
    channels, fine_cells = inc_fine.shape
    rows, pairs = pair_owner.shape
    cells = prior.shape[2]
    fblocks = fine_cells // LANES
    cap = max(2, (2 * rows * pairs + tiles - 1) // tiles)
    cap = min(cap, rows)
    slots = round_up(cap, 16)
    part = -(-channels // mems)
    fine_pad = round_up(fblocks, LANES)
    row_pad = round_up(rows, 16)
    vmem = pl.BlockSpec(memory_space=pltpu.VMEM)
    hbm = pl.BlockSpec(memory_space=pltpu.HBM)
    dma = pltpu.SemaphoreType.DMA
    small = pl.pallas_call(
        functools.partial(kernel, tiles, mems, cap),
        out_shape=pltpu.VMEM((3, SUB, cells), f32),
        in_specs=[hbm] * 8,
        out_specs=vmem,
        scratch_shapes=[
            pltpu.VMEM(inc_fine.shape, bf16),
            pltpu.VMEM((3, pairs, rows), jnp.int32),
            pltpu.VMEM((rows, LANES), f32),
            pltpu.VMEM(pair_weight.shape, bf16),
            pltpu.VMEM(prior.shape, bf16),
            pltpu.VMEM(posterior.shape, bf16),
            pltpu.VMEM((fblocks * SUB, LANES), f32),
            pltpu.VMEM((fine_pad, part * LANES), bf16),
            pltpu.VMEM((rows, LANES), f32),
            pltpu.VMEM((LANES, LANES), f32),
            pltpu.VMEM((tiles * slots, fine_pad), bf16),
            pltpu.VMEM((tiles, 1, LANES), f32),
            pltpu.VMEM((tiles, 1, LANES), f32),
            pltpu.VMEM((pairs * row_pad, tiles * slots), bf16),
            pltpu.VMEM((tiles * slots, part * LANES), bf16),
            pltpu.VMEM((tiles * slots, part * LANES), bf16),
            pltpu.VMEM((pairs, rows * SUB, LANES), f32),
            pltpu.VMEM((rows * SUB, LANES), f32),
            pltpu.VMEM((mems, pairs, round_up(rows // mems, SUB), LANES), f32),
            pltpu.VMEM((mems, 4 * SUB, cells), f32),
            pltpu.VMEM((mems, SUB, cells), f32),
            pltpu.VMEM((tiles, 1, LANES), f32),
            pltpu.VMEM((mems, 1, LANES), f32),
            dma((8,)),
            dma,
            dma,
            dma,
            dma,
            dma((mems,)),
            dma((mems,)),
            dma((2, mems)),
            dma((2, mems)),
            dma,
            dma,
            dma((mems,)),
            dma((mems,)),
            dma((mems,)),
            dma((mems,)),
        ],
        compiler_params=pltpu.CompilerParams(
            collective_id=0, has_side_effects=True, vmem_limit_bytes=56 * 1024 * 1024
        ),
        name="remap_and_spread",
    )(
        inc_fine,
        pair_owner.T,
        pair_block.T,
        pair_count.T,
        cell_area.reshape(rows, -1),
        pair_weight,
        prior,
        posterior,
    )
    center, factor, post_mean = (small[i, :channels, None, :] for i in range(3))
    return (center + factor * (posterior.astype(f32) - post_mean)).astype(bf16)


def solution(mesh):
    in_specs = (
        P(None, "tile"),
        P("tile", None),
        P("tile", None),
        P("tile", None),
        P("tile", None, None, None),
        P("tile"),
        P(None, "mem", "tile"),
        P(None, "mem", "tile"),
    )
    out_specs = P(None, "mem", "tile")
    return jax.shard_map(
        per_device, mesh=mesh, in_specs=in_specs, out_specs=out_specs, check_vma=False
    )
```

```python
import functools

import jax
import jax.numpy as jnp
from jax import lax
from jax.experimental import pallas as pl
from jax.experimental.pallas import tpu as pltpu
from jax.sharding import PartitionSpec as P

relax_weight = 0.85
variance_eps = 1e-06
f32 = jnp.float32
bf16 = jnp.bfloat16
MESH = pl.DeviceIdType.MESH
LANES = 128
SUB = 8
ONES = 7


def round_up(n, k):
    return -(-n // k) * k


def kernel(
    tiles,
    mems,
    cap,
    inc_hbm,
    owner_hbm,
    block_hbm,
    count_hbm,
    area_hbm,
    weight_hbm,
    prior_hbm,
    post_hbm,
    out_ref,
    inc_ref,
    index,
    area_ref,
    weight,
    prior,
    post,
    tall,
    fine,
    before,
    square,
    hits,
    ask,
    asked,
    pick,
    served,
    got,
    spread,
    ratio,
    shares,
    stats,
    coarse,
    level,
    whole,
    local_sem,
    ask_send,
    ask_recv,
    data_send,
    data_recv,
    stat_send,
    stat_recv,
    coarse_send,
    coarse_recv,
    level_send,
    level_recv,
    whole_send,
    whole_recv,
):
    channels = inc_ref.shape[0]
    pairs, rows = owner_hbm.shape
    fblocks = inc_ref.shape[1] // LANES
    fine_pad = fine.shape[0]
    part = got.shape[1] // LANES
    slots = got.shape[0] // tiles
    row_pad = pick.shape[0] // pairs
    members, cells = prior.shape[1], prior.shape[2]
    me = lax.axis_index("tile")
    core = lax.axis_index("mem")
    first = jnp.minimum(core * part, channels - part)

    def wrap(n, size):
        return jnp.where(n >= size, n - size, n)

    def for_all(size, action):
        def body(k, carry):
            action(k)
            return carry

        lax.fori_loop(1, size, body, 0)

    loads = [
        pltpu.make_async_copy(source, target, local_sem.at[i])
        for i, (source, target) in enumerate(
            [
                (owner_hbm, index.at[0]),
                (block_hbm, index.at[1]),
                (count_hbm, index.at[2]),
                (inc_hbm, inc_ref),
                (prior_hbm, prior),
                (weight_hbm, weight),
                (post_hbm, post),
                (area_hbm, area_ref),
            ]
        )
    ]
    for load in loads[:4]:
        load.start()

    barrier = pltpu.get_barrier_semaphore()

    def greet(tile, mem):
        pl.semaphore_signal(barrier, inc=1, device_id=(tile, mem), device_id_type=MESH)

    for_all(tiles, lambda k: greet(wrap(me + k, tiles), core))
    for k in range(1, mems):
        greet(me, wrap(core + k, mems))
    for load in loads[4:]:
        load.start()

    lane = lax.broadcasted_iota(jnp.int32, (rows, LANES), 1).astype(f32)
    square[...] = jnp.zeros_like(square)
    for load in loads[:3]:
        load.wait()
    for i in range(3):
        square[i * SUB : i * SUB + pairs, :rows] = index[i].astype(f32)
    turned = jnp.transpose(square[...])[:rows]
    owner, block, count = (turned[:, i * SUB : i * SUB + pairs] for i in range(3))
    named = [owner[:, p : p + 1] == lane for p in range(pairs)]
    any_named = jnp.zeros((rows, LANES), f32)
    wanted = jnp.zeros((rows, LANES), f32)
    for p in range(pairs):
        any_named = any_named + jnp.where(named[p], 1.0, 0.0)
        wanted = wanted + jnp.where(named[p], block[:, p : p + 1] + 1.0, 0.0)
    run = jnp.zeros((1, LANES), f32)
    for r in range(rows):
        before[r : r + 1, :] = run
        run = run + any_named[r : r + 1, :]
    earlier = before[...]
    square[...] = jnp.zeros_like(square)
    for s in range(cap):
        chosen = jnp.where((earlier == float(s)) & (any_named > 0.0), wanted, 0.0)
        square[s : s + 1, :] = jnp.sum(chosen, axis=0, keepdims=True)
    turned = jnp.transpose(square[...]) - 1.0
    for t in range(tiles):
        ask[t] = turned[t : t + 1, :]

    pl.semaphore_wait(barrier, tiles + mems - 2)

    def start_ask(k):
        other = wrap(me + k, tiles)
        pltpu.make_async_remote_copy(
            src_ref=ask.at[other],
            dst_ref=asked.at[me],
            send_sem=ask_send,
            recv_sem=ask_recv,
            device_id=(other, core),
            device_id_type=MESH,
        ).start()

    for_all(tiles, start_ask)
    asked[pl.ds(me, 1)] = ask[pl.ds(me, 1)]

    loads[3].wait()
    for b in range(fblocks):
        tall[b * SUB : b * SUB + channels, :] = inc_ref[:, b * LANES : (b + 1) * LANES].astype(f32)
    fine[...] = jnp.zeros_like(fine)
    planes = [tall[pl.ds(c, fblocks, stride=SUB), :] for c in range(channels)]
    for k in range(part):
        value = planes[k]
        for c in range(1, channels):
            value = jnp.where(first + k == c, planes[c], value)
        fine[:fblocks, k * LANES : (k + 1) * LANES] = value.astype(bf16)

    wide = lax.broadcasted_iota(jnp.int32, (rows, tiles * slots), 1).astype(f32)
    pick[...] = jnp.zeros_like(pick)
    for p in range(pairs):
        slot = jnp.sum(jnp.where(named[p], earlier, 0.0), axis=1, keepdims=True)
        place = owner[:, p : p + 1] * float(slots) + slot
        pick[p * row_pad : p * row_pad + rows, :] = jnp.where(wide == place, 1.0, 0.0).astype(bf16)

    live = [lane < count[:, p : p + 1] for p in range(pairs)]
    spread[...] = jnp.zeros_like(spread)
    ratio[...] = jnp.zeros_like(ratio)
    for p in range(pairs):
        spread[p, pl.ds(ONES, rows, stride=SUB), :] = jnp.where(live[p], 1.0, 0.0)

    chunk = next(n for n in (512, 384, 256, 128) if cells % n == 0)
    sub = lax.broadcasted_iota(jnp.int32, (SUB, chunk), 0)

    def member_stats(ref, base):
        def body(j, carry):
            at = pl.ds(pl.multiple_of(j * chunk, chunk), chunk)
            sums = jnp.zeros((SUB, chunk), f32)
            squares = jnp.zeros((SUB, chunk), f32)
            for c in range(channels):
                values = ref[c, :, at].astype(f32)
                total = jnp.sum(values, axis=0, keepdims=True)
                dev = values - total * (1.0 / members)
                sq = jnp.sum(dev * dev, axis=0, keepdims=True)
                sums = jnp.where(sub == c, total, sums)
                squares = jnp.where(sub == c, sq, squares)
            stats[core, base : base + SUB, at] = sums
            stats[core, base + SUB : base + 2 * SUB, at] = squares
            return carry

        lax.fori_loop(0, cells // chunk, body, 0)

    def wait_all(buffer, sem):
        pltpu.make_async_copy(buffer, buffer, sem).wait()

    loads[4].wait()
    member_stats(prior, 0)

    wait_all(asked.at[: tiles - 1], ask_recv)
    square[...] = jnp.zeros_like(square)
    for t in range(tiles):
        square[t : t + 1, :] = asked[t]
    turned = jnp.transpose(square[...])
    fine_lane = lax.broadcasted_iota(jnp.int32, (slots, fine_pad), 1).astype(f32)
    for t in range(tiles):
        hits[t * slots : (t + 1) * slots, :] = jnp.where(
            turned[:slots, t : t + 1] == fine_lane, 1.0, 0.0
        ).astype(bf16)
    served[...] = jnp.dot(hits[...], fine[...], preferred_element_type=f32).astype(bf16)

    def rows_of(t):
        return pl.ds(pl.multiple_of(t * slots, slots), slots)

    def start_data(k):
        other = wrap(me + k, tiles)
        pltpu.make_async_remote_copy(
            src_ref=served.at[rows_of(other)],
            dst_ref=got.at[rows_of(me)],
            send_sem=data_send,
            recv_sem=data_recv,
            device_id=(other, core),
            device_id_type=MESH,
        ).start()

    for_all(tiles, start_data)
    got[rows_of(me), :] = served[rows_of(me), :]

    loads[6].wait()
    member_stats(post, 2 * SUB)

    def core_copy(buffer, send, recv, k, here):
        other = wrap(core + k, mems)
        source = here if here is not None else other
        return pltpu.make_async_remote_copy(
            src_ref=buffer.at[core],
            dst_ref=buffer.at[source],
            send_sem=send.at[other],
            recv_sem=recv.at[source],
            device_id=(me, other),
            device_id_type=MESH,
        )

    for k in range(1, mems):
        core_copy(stats, stat_send, stat_recv, k, core).start()

    loads[5].wait()
    loads[7].wait()

    def remap(r):
        left = jnp.concatenate(
            [spread[p, r * SUB : (r + 1) * SUB, :] for p in range(pairs)], axis=1
        ).astype(bf16)
        right = jnp.concatenate([weight[r, p] for p in range(pairs)], axis=1)
        return lax.dot_general(
            left, right, (((1,), (1,)), ((), ())), preferred_element_type=f32
        )

    for r in range(rows):
        before[r : r + 1, :] = remap(r)[ONES : ONES + 1, :]
    rest = area_ref[...] / before[...]
    for i in range(3):
        rounded = rest.astype(bf16).astype(f32)
        ratio[pl.ds(i, rows, stride=SUB), :] = rounded
        rest = rest - rounded
    for r in range(rows):
        right = jnp.concatenate([weight[r, p] for p in range(pairs)], axis=1)
        share = jnp.dot(
            ratio[r * SUB : (r + 1) * SUB, :].astype(bf16), right, preferred_element_type=f32
        )
        share = jnp.sum(share, axis=0, keepdims=True)
        for p in range(pairs):
            shares[p, r : r + 1, :] = share[:, p * LANES : (p + 1) * LANES]

    for k in range(1, mems):
        core_copy(stats, stat_send, stat_recv, k, None).wait()
    everyone = members * mems
    for j in range(cells // chunk):
        at = slice(j * chunk, (j + 1) * chunk)

        def combined(base):
            sums = [stats[m, base : base + SUB, at] for m in range(mems)]
            mean = functools.reduce(jnp.add, sums) * (1.0 / everyone)
            total = functools.reduce(
                jnp.add, [stats[m, base + SUB : base + 2 * SUB, at] for m in range(mems)]
            )
            for s in sums:
                off = s * (1.0 / members) - mean
                total = total + members * (off * off)
            return mean, jnp.sqrt(total * (1.0 / (everyone - 1)) + variance_eps)

        prior_mean, prior_spread = combined(0)
        post_mean, post_spread = combined(2 * SUB)
        out_ref[0, :, at] = prior_mean
        out_ref[1, :, at] = 1.0 + relax_weight * (prior_spread - post_spread) / post_spread
        out_ref[2, :, at] = post_mean

    wait_all(got.at[: (tiles - 1) * slots], data_recv)
    picked = jnp.dot(pick[...], got[...], preferred_element_type=f32)
    level_lane = lax.broadcasted_iota(jnp.int32, (1, LANES), 1)
    row = jnp.where(level_lane == ONES, jnp.sum(area_ref[...], keepdims=True), 0.0)
    for k in range(part):
        added = jnp.zeros((rows, LANES), f32)
        for p in range(pairs):
            mine = picked[p * row_pad : p * row_pad + rows, k * LANES : (k + 1) * LANES]
            added = added + jnp.where(live[p], mine * shares[p], 0.0)
        here = (level_lane == first + k) & (core * part < channels)
        row = jnp.where(here, jnp.sum(added, keepdims=True), row)
    level[pl.ds(me, 1)] = row[None]

    def start_level(k):
        pltpu.make_async_remote_copy(
            src_ref=level.at[me],
            dst_ref=level.at[me],
            send_sem=level_send,
            recv_sem=level_recv,
            device_id=(wrap(me + k, tiles), core),
            device_id_type=MESH,
        ).start()

    for_all(tiles, start_level)

    for p in range(pairs):
        for c in range(channels):
            value = jnp.zeros((rows, LANES), f32)
            for k in range(part):
                mine = picked[p * row_pad : p * row_pad + rows, k * LANES : (k + 1) * LANES]
                value = jnp.where((first + k == c) & (core * part < channels), mine, value)
            spread[p, pl.ds(c, rows, stride=SUB), :] = jnp.where(live[p], value, 0.0)

    pieces = 2
    piece = rows // pieces

    def coarse_copy(i, k, here):
        other = wrap(core + k, mems)
        source = here if here is not None else other
        at = pl.ds(i * piece * LANES, piece * LANES)
        return pltpu.make_async_remote_copy(
            src_ref=coarse.at[core, :, at],
            dst_ref=coarse.at[source, :, at],
            send_sem=coarse_send.at[i, other],
            recv_sem=coarse_recv.at[i, source],
            device_id=(me, other),
            device_id_type=MESH,
        )

    for i in range(pieces):
        for r in range(i * piece, (i + 1) * piece):
            product = remap(r)
            coarse[core, :, r * LANES : (r + 1) * LANES] = product / product[ONES : ONES + 1, :]
        for k in range(1, mems):
            coarse_copy(i, k, core).start()

    wait_all(level.at[: tiles - 1], level_recv)
    row = level[0]
    for t in range(1, tiles):
        row = row + level[t]
    whole[pl.ds(core, 1)] = row[None]
    for k in range(1, mems):
        core_copy(whole, whole_send, whole_recv, k, core).start()
    for i in range(pieces):
        for k in range(1, mems):
            coarse_copy(i, k, None).wait()
    for k in range(1, mems):
        core_copy(whole, whole_send, whole_recv, k, None).wait()
    row = whole[0]
    for m in range(1, mems):
        row = row + whole[m]
    eye = lax.broadcasted_iota(jnp.int32, (SUB, LANES), 0) == lax.broadcasted_iota(
        jnp.int32, (SUB, LANES), 1
    )
    weighted = jnp.sum(jnp.where(eye, row, 0.0), axis=1, keepdims=True)
    area = weighted[ONES : ONES + 1, :] * (1.0 / mems)
    mean = weighted / area
    for j in range(cells // chunk):
        at = slice(j * chunk, (j + 1) * chunk)
        value = functools.reduce(jnp.add, [coarse[m, :, at] for m in range(mems)])
        out_ref[0, :, at] = out_ref[0, :, at] + (value - mean)
    wait_all(asked.at[: tiles - 1], ask_send)
    wait_all(got.at[: (tiles - 1) * slots], data_send)
    wait_all(level.at[: tiles - 1], level_send)


def per_device(
    inc_fine, pair_owner, pair_block, pair_count, pair_weight, cell_area, prior, posterior
):
    tiles = lax.axis_size("tile")
    mems = lax.axis_size("mem")
    channels, fine_cells = inc_fine.shape
    rows, pairs = pair_owner.shape
    cells = prior.shape[2]
    fblocks = fine_cells // LANES
    cap = max(2, (2 * rows * pairs + tiles - 1) // tiles)
    cap = min(cap, rows)
    slots = round_up(cap, 16)
    part = -(-channels // mems)
    fine_pad = round_up(fblocks, LANES)
    row_pad = round_up(rows, 16)
    vmem = pl.BlockSpec(memory_space=pltpu.VMEM)
    hbm = pl.BlockSpec(memory_space=pltpu.HBM)
    dma = pltpu.SemaphoreType.DMA
    small = pl.pallas_call(
        functools.partial(kernel, tiles, mems, cap),
        out_shape=pltpu.VMEM((3, SUB, cells), f32),
        in_specs=[hbm] * 8,
        out_specs=vmem,
        scratch_shapes=[
            pltpu.VMEM(inc_fine.shape, bf16),
            pltpu.VMEM((3, pairs, rows), jnp.int32),
            pltpu.VMEM((rows, LANES), f32),
            pltpu.VMEM(pair_weight.shape, bf16),
            pltpu.VMEM(prior.shape, bf16),
            pltpu.VMEM(posterior.shape, bf16),
            pltpu.VMEM((fblocks * SUB, LANES), f32),
            pltpu.VMEM((fine_pad, part * LANES), bf16),
            pltpu.VMEM((rows, LANES), f32),
            pltpu.VMEM((LANES, LANES), f32),
            pltpu.VMEM((tiles * slots, fine_pad), bf16),
            pltpu.VMEM((tiles, 1, LANES), f32),
            pltpu.VMEM((tiles, 1, LANES), f32),
            pltpu.VMEM((pairs * row_pad, tiles * slots), bf16),
            pltpu.VMEM((tiles * slots, part * LANES), bf16),
            pltpu.VMEM((tiles * slots, part * LANES), bf16),
            pltpu.VMEM((pairs, rows * SUB, LANES), f32),
            pltpu.VMEM((rows * SUB, LANES), f32),
            pltpu.VMEM((pairs, rows, LANES), f32),
            pltpu.VMEM((mems, 4 * SUB, cells), f32),
            pltpu.VMEM((mems, SUB, cells), f32),
            pltpu.VMEM((tiles, 1, LANES), f32),
            pltpu.VMEM((mems, 1, LANES), f32),
            dma((8,)),
            dma,
            dma,
            dma,
            dma,
            dma((mems,)),
            dma((mems,)),
            dma((2, mems)),
            dma((2, mems)),
            dma,
            dma,
            dma((mems,)),
            dma((mems,)),
        ],
        compiler_params=pltpu.CompilerParams(
            collective_id=0, has_side_effects=True, vmem_limit_bytes=56 * 1024 * 1024
        ),
        name="remap_and_spread",
    )(
        inc_fine,
        pair_owner.T,
        pair_block.T,
        pair_count.T,
        cell_area.reshape(rows, -1),
        pair_weight,
        prior,
        posterior,
    )
    center, factor, post_mean = (small[i, :channels, None, :] for i in range(3))
    return (center + factor * (posterior.astype(f32) - post_mean)).astype(bf16)


def solution(mesh):
    in_specs = (
        P(None, "tile"),
        P("tile", None),
        P("tile", None),
        P("tile", None),
        P("tile", None, None, None),
        P("tile"),
        P(None, "mem", "tile"),
        P(None, "mem", "tile"),
    )
    out_specs = P(None, "mem", "tile")
    return jax.shard_map(
        per_device, mesh=mesh, in_specs=in_specs, out_specs=out_specs, check_vma=False
    )
```
